512 devices in a mesh: group: 16 (over y, x), pos: 32 (over z, core).
Axes of the slice: x: 4, y: 4, z: 16, core: 2. Of those that a mesh axis runs over, the one named last changes fastest.
Arguments:
- queries: bfloat16 [65536, 256], P(('group', 'pos')), parts along dimension 0, may hold values from -24 to 24
- hist_keys: bfloat16 [524288, 256], P(('group', 'pos')), parts along dimension 0, may hold values from -24 to 24
- hist_values: bfloat16 [524288, 256], P(('group', 'pos')), parts along dimension 0, may hold values from -6 to 6
- block_dev: int32 [65536, 8], P(('group', 'pos')), parts along dimension 0, may hold values from 0 to 31, all different within a row; in each aligned block of 128 rows (0 to 127, 128 to 255, ...) at most 64 rows name the same one
- block_local: int32 [65536, 8], P(('group', 'pos')), parts along dimension 0, may hold values from 0 to 7
Outputs:
- attended: bfloat16 [65536, 256], P(('group', 'pos')), parts along dimension 0
The draws below stay inside these ranges and needn't reach their ends.
There are 16 independent parts, one for each index of `group`. The reference program is written for one: setup_inputs(seed, part) draws one part's arguments, and reference() takes and returns one part's arrays. A program takes and returns all parts, laid end to end along the dimension named above; each array names one. Nothing has to cross between parts.
Inputs may be any that keep to these rules, and one draw needn't show every extreme that they name: `block_dev`: each candidate names 8 different devices. Among the candidates of one device at most 64 name the same device, and in every draw some device is named by exactly 64 of them.
All inputs are finite; a program needn't handle non-finite values.
Results may differ from the reference program's by a relative error of at most 0.0055.
Values may be sent and summed in bfloat16 or wider, within the bound.
No kernel may reach another device: no remote copies, remote signals or barrier semaphores. Data moves between devices by JAX's collectives and lax.ppermute only.
A program may use at most 64 MiB of HBM per device.

```python
import math
import jax
import jax.numpy as jnp
import numpy as np
from jax import lax

D = 256
BLK = 128
TOPK = 8
HB_DEV = 8
CAND_DEV = 128
CAND = 4096
HIST = 32768
CAP = 64
N_POS = 32


def draw_queries(key, part):
    key = jax.random.fold_in(key, 11)
    first = jax.random.fold_in(key, 0)
    noise = jax.random.normal(first, (CAND, D), jnp.float32)
    return jnp.clip(noise, -24.0, 24.0).astype(jnp.bfloat16)


def draw_hist_keys(key, part):
    key = jax.random.fold_in(key, 23)
    first = jax.random.fold_in(key, 0)
    noise = jax.random.normal(first, (HIST, D), jnp.float32)
    return jnp.clip(noise, -24.0, 24.0).astype(jnp.bfloat16)


def with_ends(values, stream_key, smallest, top_value):
    dims = values.shape
    spot = [jax.random.randint(jax.random.fold_in(stream_key, axis), (), 0, dims[axis]) for axis in range(len(dims))]
    values = values.at[tuple(spot)].set(smallest)
    longest = dims.index(max(dims))
    spot[longest] = (spot[longest] + 1) % dims[longest]
    return values.at[tuple(spot)].set(top_value)


def block_scale(key, dims, pieces, low, high):
    gain = 1.0
    for dim, blocks in pieces:
        draws = jax.random.uniform(jax.random.fold_in(jax.random.fold_in(key, 6), dim), (blocks,), jnp.float32, low / len(pieces), high / len(pieces))
        gain = gain * jnp.repeat(jnp.exp(draws), dims[dim] // blocks).reshape((-1,) + (1,) * (len(dims) - 1 - dim))
    return gain


def assign_block(own_key, own, number, rows, number_of, top, reach, skew):
    order = jax.random.permutation(own_key, number_of)
    packed, usual = portions_of(number_of, rows * top, reach, skew, True), portions_of(number_of, rows * top, reach, skew, False)
    places = jnp.arange(number_of)

    def named(sizes, rotation):
        used = int((sizes > 0).sum())
        fixed = max(1, used // 4)
        shifted = fixed + (places - fixed + rotation * (used - fixed)) % max(1, number_of - fixed)
        return jnp.zeros((number_of,), jnp.int32).at[order[jnp.where(places < fixed, places, shifted)]].set(jnp.asarray(sizes, jnp.int32))

    sizes = jnp.where(number % 4 == 0, named(packed, number // 4), named(usual, number - number // 4 - 1))
    mixed = jax.random.permutation(jax.random.fold_in(own, 3), number_of)
    source_of, taker = mixed[0:number_of // 2 * 2:2], mixed[1:number_of // 2 * 2:2]
    slack = jnp.minimum(sizes[source_of] - 1, reach - sizes[taker]) // 2
    slack = jnp.where((source_of == order[0]) | (taker == order[0]) | (sizes[taker] == 0), 0, jnp.maximum(slack, 0))
    shifted = jax.random.randint(jax.random.fold_in(own, 4), (number_of // 2,), 0, 1 << 20) % (slack + 1)
    sizes = sizes.at[source_of].add(-shifted).at[taker].add(shifted)
    labels = jnp.searchsorted(jnp.cumsum(sizes), jnp.arange(rows * top), side="right").astype(jnp.int32)
    listing = labels.reshape(top, rows).T
    listing = listing[jax.random.permutation(jax.random.fold_in(own, 1), rows)]
    rotation = jax.random.randint(jax.random.fold_in(own, 2), (rows, 1), 0, top)
    return jnp.take_along_axis(listing, (jnp.arange(top)[None, :] + rotation) % top, axis=1)


def portions_of(count, total, most, slope, full):
    portions = [(1 << 20) // math.isqrt(standing ** slope) + 1 for standing in range(1, count + 1)]
    largest = most if full else min(most, max(-(-total // count), total * portions[0] // sum(portions)))
    least = 1 if total - largest >= count - 1 else 0
    holding, spare = [largest] + [least] * (count - 1), total - largest - least * (count - 1)
    while spare > 0:
        free = [i for i in range(1, count) if holding[i] < largest] or [i for i in range(1, count) if holding[i] < most]
        pool, left = sum([portions[i] for i in free]), spare
        for i in free:
            addition = min(most - holding[i], max(1, left * portions[i] // pool), spare)
            holding[i] = holding[i] + addition
            spare = spare - addition
    return np.array(holding)


def scatter_about(stream_key, shape, width, most, cuts=(), kind=jnp.bfloat16):
    array = jax.random.normal(stream_key, shape, jnp.float32) * width
    if len(cuts) > 0:
        array = block_scale(stream_key, shape, cuts, -0.22, 0.18) * array
    return jnp.clip(array, min=-most, max=most).astype(kind)


def setup_inputs(seed: int = 0, part: int = 0) -> dict:
    splits = jax.random.split(jax.random.key(seed), 6)
    part_splits = jax.random.split(jax.random.fold_in(splits[5], part), 6)
    queries = draw_queries(jax.random.fold_in(jax.random.fold_in(splits[5], part), 71), part)
    hist_keys = draw_hist_keys(jax.random.fold_in(jax.random.fold_in(splits[5], part), 71), part)
    hist_values = scatter_about(part_splits[2], (HIST, D), 1.0, 6.0, ((0, 32),))
    block_dev_keys = jax.random.split(jax.random.fold_in(part_splits[3], 1), CAND // CAND_DEV)
    block_dev_turns = jax.random.permutation(jax.random.fold_in(part_splits[3], 3), CAND // CAND_DEV)
    block_dev = jax.vmap(lambda own, number: assign_block(jax.random.fold_in(part_splits[3], 2), own, number, CAND_DEV, N_POS, TOPK, CAP, 2))(block_dev_keys, block_dev_turns).reshape((CAND, TOPK))
    block_local = with_ends(jax.random.randint(part_splits[4], (CAND, TOPK), 0, HB_DEV), jax.random.fold_in(part_splits[4], 1), 0, HB_DEV - 1).astype(jnp.int32)
    return dict(queries=queries, hist_keys=hist_keys, hist_values=hist_values, block_dev=block_dev, block_local=block_local)


def reference(queries, hist_keys, hist_values, block_dev, block_local):
    keys = hist_keys.reshape(N_POS * HB_DEV, BLK, D)
    vals = hist_values.reshape(N_POS * HB_DEV, BLK, D)
    blocks = (block_dev * HB_DEV + block_local).astype(jnp.int32)
    size = 64 if CAND % 64 == 0 else CAND
    scale = 1.0 / (D ** 0.5)

    def one(args):
        query, index = args
        kblock = keys[index].astype(jnp.float32)
        vblock = vals[index].astype(jnp.float32)
        scores = jnp.einsum("gd,gkbd->gkb", query.astype(jnp.float32), kblock) * scale
        peak = jnp.max(scores, axis=-1)
        expo = jnp.exp(scores - peak[..., None])
        total = jnp.sum(expo, axis=-1)
        weights = lax.optimization_barrier(expo.astype(jnp.bfloat16)).astype(jnp.float32)
        partial_value = (jnp.einsum("gkb,gkbd->gkd", weights, vblock) / total[..., None]).astype(jnp.bfloat16)
        partial_value = lax.optimization_barrier(partial_value).astype(jnp.float32)
        lse = peak + jnp.log(total)
        top = jnp.max(lse, axis=-1, keepdims=True)
        mix = jnp.exp(lse - top)
        mix = mix / jnp.sum(mix, axis=-1, keepdims=True)
        return jnp.sum(mix[..., None] * partial_value, axis=1).astype(jnp.bfloat16)

    result = lax.map(one, (queries.reshape(CAND // size, size, D), blocks.reshape(CAND // size, size, TOPK)))
    return result.reshape(CAND, D)
```

```python
import functools

import jax
import jax.numpy as jnp
from jax import lax
from jax.experimental import pallas as pl
from jax.experimental.pallas import tpu as pltpu
from jax.sharding import Mesh, PartitionSpec as P

BLK = 128
NONE = -1e30


def attend_kernel(nloc, chip_ref, x_ref, k_ref, vt_ref, out_ref):
    cand = out_ref.shape[2]
    width = k_ref.shape[2]
    first = (chip_ref[0] * (2 * nloc)).astype(jnp.float32)
    query = jnp.concatenate([x_ref[0, :cand, :], x_ref[1, :cand, :]], axis=0)
    ids = jnp.concatenate(
        [x_ref[0, cand:, :cand].astype(jnp.float32), x_ref[1, cand:, :cand].astype(jnp.float32)],
        axis=1,
    )
    scale = 1.0 / width**0.5
    parts, lses = [], []
    for half in range(2):
        near = ids - (first + half * nloc)
        inside = jnp.logical_and(near >= 0.0, near < nloc)
        sel = jnp.max(jnp.where(inside, near, -1.0), axis=0, keepdims=True)
        scores = lax.dot_general(
            k_ref[half], query, (((1,), (1,)), ((), ())), preferred_element_type=jnp.float32
        )
        picked = scores[0:BLK]
        for b in range(1, nloc):
            picked = jnp.where(sel == b, scores[b * BLK : (b + 1) * BLK], picked)
        peak = jnp.max(picked, axis=0, keepdims=True)
        expo = jnp.exp((picked - peak) * scale)
        total = jnp.sum(expo, axis=0, keepdims=True)
        spread = jnp.concatenate(
            [jnp.where(sel == b, expo, 0.0).astype(jnp.bfloat16) for b in range(nloc)], axis=0
        )
        summed = jnp.dot(vt_ref[half], spread, preferred_element_type=jnp.float32)
        parts.append((summed / total).astype(jnp.bfloat16).astype(jnp.float32))
        lses.append(jnp.where(sel >= 0.0, peak * scale + jnp.log(total), NONE))
    top = jnp.maximum(lses[0], lses[1])
    mix0, mix1 = jnp.exp(lses[0] - top), jnp.exp(lses[1] - top)
    mixed = mix0 + mix1
    merged = ((mix0 / mixed) * parts[0] + (mix1 / mixed) * parts[1]).astype(jnp.bfloat16)
    lse = top + jnp.log(mixed)
    big = lse.astype(jnp.bfloat16)
    rest = lse - big.astype(jnp.float32)
    mid = rest.astype(jnp.bfloat16)
    low = (rest - mid.astype(jnp.float32)).astype(jnp.bfloat16)
    row = lax.broadcasted_iota(jnp.int32, (16, 2 * cand), 0)
    tail = jnp.where(
        row == 0,
        big.astype(jnp.float32),
        jnp.where(row == 1, mid.astype(jnp.float32), low.astype(jnp.float32)),
    ).astype(jnp.bfloat16)
    for s in range(2):
        out_ref[s, :width, :] = merged[:, s * cand : (s + 1) * cand]
        out_ref[s, width:, :] = tail[:, s * cand : (s + 1) * cand]


def attend(chip, x, keys, vt, cand):
    sources, rows, width = x.shape
    halves, positions, _ = keys.shape
    return pl.pallas_call(
        functools.partial(attend_kernel, positions // BLK),
        grid=(sources // 2,),
        in_specs=[
            pl.BlockSpec(memory_space=pltpu.SMEM),
            pl.BlockSpec((2, rows, width), lambda i: (i, 0, 0)),
            pl.BlockSpec((halves, positions, width), lambda i: (0, 0, 0)),
            pl.BlockSpec((halves, width, positions), lambda i: (0, 0, 0)),
        ],
        out_specs=pl.BlockSpec((2, width + 16, cand), lambda i: (i, 0, 0)),
        out_shape=jax.ShapeDtypeStruct((sources, width + 16, cand), jnp.bfloat16),
        compiler_params=pltpu.CompilerParams(vmem_limit_bytes=40 * 1024 * 1024),
    )(chip, x, keys, vt)


def merge_kernel(x_ref, out_ref):
    sources, rows, cand = x_ref.shape
    width = rows - 16
    lses = []
    for s in range(sources):
        tail = x_ref[s, width:, :].astype(jnp.float32)
        lses.append(tail[0:1] + tail[1:2] + tail[2:3])
    top = functools.reduce(jnp.maximum, lses)
    mixes = [jnp.exp(one - top) for one in lses]
    inverse = 1.0 / functools.reduce(jnp.add, mixes)
    total = jnp.zeros((width, cand), jnp.float32)
    for s in range(sources):
        total = total + (mixes[s] * inverse) * x_ref[s, :width, :].astype(jnp.float32)
    out_ref[...] = total.T.astype(jnp.bfloat16)


def merge(x):
    _, rows, cand = x.shape
    return pl.pallas_call(
        merge_kernel,
        out_shape=jax.ShapeDtypeStruct((cand, rows - 16), jnp.bfloat16),
        compiler_params=pltpu.CompilerParams(vmem_limit_bytes=40 * 1024 * 1024),
    )(x)


def body(queries, hist_keys, hist_values, block_dev, block_local):
    chips = lax.axis_size("z")
    cand, width = queries.shape
    nloc = hist_keys.shape[0] // BLK
    topk = block_dev.shape[1]
    ids = (block_dev * nloc + block_local).astype(jnp.bfloat16).T
    mine = jnp.concatenate([queries, jnp.pad(ids, ((0, 0), (0, width - cand)))], axis=0)
    x = lax.all_to_all(
        jnp.broadcast_to(mine[None], (chips, cand + topk, width)), "z", 0, 0, tiled=True
    )
    core = lax.axis_index("core")
    other_keys = lax.ppermute(hist_keys, "core", [(0, 1), (1, 0)])
    vt = hist_values.T
    other_vt = lax.ppermute(vt, "core", [(0, 1), (1, 0)])
    keys = jnp.where(core == 0, jnp.stack([hist_keys, other_keys]), jnp.stack([other_keys, hist_keys]))
    vts = jnp.where(core == 0, jnp.stack([vt, other_vt]), jnp.stack([other_vt, vt]))
    chip = lax.axis_index("z").astype(jnp.int32).reshape(1)
    sent = attend(chip, x, keys, vts, cand)
    back = lax.all_to_all(sent, "z", 0, 0, tiled=True)
    return merge(back)


def solution(mesh):
    groups, pos = mesh.devices.shape
    chips = Mesh(mesh.devices.reshape(groups, pos // 2, 2), ("group", "z", "core"))
    spec = P(("group", "z", "core"), None)
    return jax.shard_map(
        body, mesh=chips, in_specs=(spec,) * 5, out_specs=spec, check_vma=False
    )
```

```python
import functools

import jax
import jax.numpy as jnp
from jax import lax
from jax.experimental import pallas as pl
from jax.experimental.pallas import tpu as pltpu
from jax.sharding import Mesh, PartitionSpec as P

BLK = 128
NONE = -1e30
TAIL = 16
VMEM = pl.BlockSpec(memory_space=pltpu.VMEM)
SMEM = pl.BlockSpec(memory_space=pltpu.SMEM)
PARAMS = pltpu.CompilerParams(vmem_limit_bytes=40 * 1024 * 1024)


def tail_rows(lse):
    big = lse.astype(jnp.bfloat16).astype(jnp.float32)
    rest = lse - big
    mid = rest.astype(jnp.bfloat16).astype(jnp.float32)
    row = lax.broadcasted_iota(jnp.int32, (TAIL, lse.shape[1]), 0)
    return jnp.where(row == 0, big, jnp.where(row == 1, mid, rest - mid)).astype(jnp.bfloat16)


def lse_row(tail):
    tail = tail.astype(jnp.float32)
    return tail[0:1] + tail[1:2] + tail[2:3]


def attend_kernel(first_ref, x_ref, k0_ref, k1_ref, v0_ref, v1_ref, out_ref):
    sources, _, cand = out_ref.shape
    positions, width = k0_ref.shape
    nloc = positions // BLK
    scale = 1.0 / width**0.5
    for s in range(0, sources, 2):
        query = jnp.concatenate([x_ref[s, :cand, :], x_ref[s + 1, :cand, :]], axis=0)
        ids = jnp.concatenate(
            [
                x_ref[s, cand:, :cand].astype(jnp.float32),
                x_ref[s + 1, cand:, :cand].astype(jnp.float32),
            ],
            axis=1,
        )
        parts, lses = [], []
        for half, (k_ref, v_ref) in enumerate(((k0_ref, v0_ref), (k1_ref, v1_ref))):
            near = ids - first_ref[half].astype(jnp.float32)
            inside = jnp.logical_and(near >= 0.0, near < nloc)
            sel = jnp.max(jnp.where(inside, near, -1.0), axis=0, keepdims=True)
            scores = lax.dot_general(
                k_ref[...], query, (((1,), (1,)), ((), ())), preferred_element_type=jnp.float32
            )
            picked = scores[0:BLK]
            for b in range(1, nloc):
                picked = jnp.where(sel == b, scores[b * BLK : (b + 1) * BLK], picked)
            peak = jnp.max(picked, axis=0, keepdims=True)
            expo = jnp.exp((picked - peak) * scale)
            total = jnp.sum(expo, axis=0, keepdims=True)
            spread = jnp.concatenate(
                [jnp.where(sel == b, expo, 0.0).astype(jnp.bfloat16) for b in range(nloc)], axis=0
            )
            summed = jnp.dot(v_ref[...], spread, preferred_element_type=jnp.float32)
            parts.append((summed / total).astype(jnp.bfloat16).astype(jnp.float32))
            lses.append(jnp.where(sel >= 0.0, peak * scale + jnp.log(total), NONE))
        top = jnp.maximum(lses[0], lses[1])
        mix0, mix1 = jnp.exp(lses[0] - top), jnp.exp(lses[1] - top)
        mixed = mix0 + mix1
        merged = ((mix0 / mixed) * parts[0] + (mix1 / mixed) * parts[1]).astype(jnp.bfloat16)
        tail = tail_rows(top + jnp.log(mixed))
        for j in range(2):
            out_ref[s + j, :width, :] = merged[:, j * cand : (j + 1) * cand]
            out_ref[s + j, width:, :] = tail[:, j * cand : (j + 1) * cand]


def attend(first, x, keys, vts, cand):
    sources, _, width = x.shape
    return pl.pallas_call(
        attend_kernel,
        in_specs=[SMEM] + [VMEM] * 5,
        out_specs=VMEM,
        out_shape=jax.ShapeDtypeStruct((sources, width + TAIL, cand), jnp.bfloat16),
        compiler_params=PARAMS,
    )(first, x, *keys, *vts)


def mix(blocks):
    width = blocks[0].shape[0] - TAIL
    lses = [lse_row(one[width:, :]) for one in blocks]
    top = functools.reduce(jnp.maximum, lses)
    mixes = [jnp.exp(one - top) for one in lses]
    mixed = functools.reduce(jnp.add, mixes)
    inverse = 1.0 / mixed
    total = (mixes[0] * inverse) * blocks[0][:width, :].astype(jnp.float32)
    for one, block in zip(mixes[1:], blocks[1:]):
        total = total + (one * inverse) * block[:width, :].astype(jnp.float32)
    return total, top + jnp.log(mixed)


def near_kernel(*refs):
    out_ref = refs[-1]
    sources, rows, _ = out_ref.shape
    for s in range(sources):
        total, lse = mix([ref[s] for ref in refs[:-1]])
        out_ref[s, : rows - TAIL, :] = total.astype(jnp.bfloat16)
        out_ref[s, rows - TAIL :, :] = tail_rows(lse)


def near_merge(*parts):
    return pl.pallas_call(
        near_kernel,
        in_specs=[VMEM] * len(parts),
        out_specs=VMEM,
        out_shape=jax.ShapeDtypeStruct(parts[0].shape, parts[0].dtype),
        compiler_params=PARAMS,
    )(*parts)


def far_kernel(x_ref, out_ref):
    total, _ = mix([x_ref[s] for s in range(x_ref.shape[0])])
    out_ref[...] = total.T.astype(jnp.bfloat16)


def far_merge(x):
    _, rows, cand = x.shape
    return pl.pallas_call(
        far_kernel,
        in_specs=[VMEM],
        out_specs=VMEM,
        out_shape=jax.ShapeDtypeStruct((cand, rows - TAIL), jnp.bfloat16),
        compiler_params=PARAMS,
    )(x)


def body(chips, queries, hist_keys, hist_values, block_dev, block_local):
    cand, width = queries.shape
    nloc = hist_keys.shape[0] // BLK
    topk = block_dev.shape[1]
    stride = 4
    members = chips // stride

    def shift(x, by):
        pairs = [
            (2 * z + c, 2 * ((z + by(c)) % chips) + c) for z in range(chips) for c in range(2)
        ]
        return lax.ppermute(x, ("z", "core"), pairs)

    far = [[2 * (r + stride * j) + c for j in range(members)] for c in range(2) for r in range(stride)]

    def exchange(x):
        return lax.all_to_all(x, ("z", "core"), 0, 0, tiled=True, axis_index_groups=far)

    swap = [(0, 1), (1, 0)]
    ids = (block_dev * nloc + block_local).astype(jnp.bfloat16).T
    mine = jnp.concatenate([queries, jnp.pad(ids, ((0, 0), (0, width - cand)))], axis=0)
    own = exchange(jnp.broadcast_to(mine[None], (members, cand + topk, width)))
    vt = hist_values.T
    keys = (hist_keys, lax.ppermute(hist_keys, "core", swap))
    vts = (vt, lax.ppermute(vt, "core", swap))
    here = 2 * lax.axis_index("z").astype(jnp.int32)
    core = lax.axis_index("core").astype(jnp.int32)
    first = jnp.stack([here + core, here + 1 - core]) * nloc

    steps = (lambda c: 2 - 4 * c, lambda c: 1, lambda c: -1)
    others = [shift(own, by) for by in steps]
    mine_part = attend(first, own, keys, vts, cand)
    back = [
        shift(attend(first, x, keys, vts, cand), lambda c, by=by: -by(c))
        for x, by in zip(others, steps)
    ]
    merged = near_merge(mine_part, *back)
    return far_merge(exchange(merged))


def solution(mesh):
    groups, pos = mesh.devices.shape
    chips = Mesh(mesh.devices.reshape(groups, pos // 2, 2), ("group", "z", "core"))
    spec = P(("group", "z", "core"), None)
    return jax.shard_map(
        functools.partial(body, pos // 2),
        mesh=chips,
        in_specs=(spec,) * 5,
        out_specs=spec,
        check_vma=False,
    )
```

```python
import functools

import jax
import jax.numpy as jnp
from jax import lax
from jax.experimental import pallas as pl
from jax.experimental.pallas import tpu as pltpu
from jax.sharding import Mesh, PartitionSpec as P

BLK = 128
NONE = -1e30
TAIL = 16
VMEM = pl.BlockSpec(memory_space=pltpu.VMEM)
SMEM = pl.BlockSpec(memory_space=pltpu.SMEM)
PARAMS = pltpu.CompilerParams(vmem_limit_bytes=40 * 1024 * 1024)


def tail_rows(lse):
    big = lse.astype(jnp.bfloat16).astype(jnp.float32)
    rest = lse - big
    mid = rest.astype(jnp.bfloat16).astype(jnp.float32)
    row = lax.broadcasted_iota(jnp.int32, (TAIL, lse.shape[1]), 0)
    return jnp.where(row == 0, big, jnp.where(row == 1, mid, rest - mid)).astype(jnp.bfloat16)


def lse_row(tail):
    tail = tail.astype(jnp.float32)
    return tail[0:1] + tail[1:2] + tail[2:3]


def attend_kernel(stride, place_ref, xa_ref, xb_ref, k0_ref, k1_ref, v0_ref, v1_ref, out_ref):
    members, _, cand = out_ref.shape
    rest = cand - xa_ref.shape[1]
    positions, width = k0_ref.shape
    nloc = positions // BLK
    scale = 1.0 / width**0.5
    for s in range(0, members, 2):
        rows, ids = [], []
        for j in range(2):
            source = place_ref[0] + stride * (s + j)
            small = xb_ref[source]
            rows += [xa_ref[source], small[:rest]]
            ids.append(small[rest:, :cand].astype(jnp.float32))
        query = jnp.concatenate(rows, axis=0)
        ids = jnp.concatenate(ids, axis=1)
        parts, lses = [], []
        for half, (k_ref, v_ref) in enumerate(((k0_ref, v0_ref), (k1_ref, v1_ref))):
            near = ids - place_ref[1 + half].astype(jnp.float32)
            inside = jnp.logical_and(near >= 0.0, near < nloc)
            sel = jnp.max(jnp.where(inside, near, -1.0), axis=0, keepdims=True)
            scores = lax.dot_general(
                k_ref[...], query, (((1,), (1,)), ((), ())), preferred_element_type=jnp.float32
            )
            picked = scores[0:BLK]
            for b in range(1, nloc):
                picked = jnp.where(sel == b, scores[b * BLK : (b + 1) * BLK], picked)
            peak = jnp.max(picked, axis=0, keepdims=True)
            expo = jnp.exp((picked - peak) * scale)
            total = jnp.sum(expo, axis=0, keepdims=True)
            spread = jnp.concatenate(
                [jnp.where(sel == b, expo, 0.0).astype(jnp.bfloat16) for b in range(nloc)], axis=0
            )
            summed = jnp.dot(v_ref[...], spread, preferred_element_type=jnp.float32)
            parts.append((summed / total).astype(jnp.bfloat16).astype(jnp.float32))
            lses.append(jnp.where(sel >= 0.0, peak * scale + jnp.log(total), NONE))
        top = jnp.maximum(lses[0], lses[1])
        mix0, mix1 = jnp.exp(lses[0] - top), jnp.exp(lses[1] - top)
        mixed = mix0 + mix1
        merged = ((mix0 / mixed) * parts[0] + (mix1 / mixed) * parts[1]).astype(jnp.bfloat16)
        tail = tail_rows(top + jnp.log(mixed))
        for j in range(2):
            out_ref[s + j, :width, :] = merged[:, j * cand : (j + 1) * cand]
            out_ref[s + j, width:, :] = tail[:, j * cand : (j + 1) * cand]


def attend(place, xa, xb, keys, vts, cand, stride):
    chips, _, width = xa.shape
    return pl.pallas_call(
        functools.partial(attend_kernel, stride),
        in_specs=[SMEM] + [VMEM] * 6,
        out_specs=VMEM,
        out_shape=jax.ShapeDtypeStruct((chips // stride, width + TAIL, cand), jnp.bfloat16),
        compiler_params=PARAMS,
    )(place, xa, xb, *keys, *vts)


def mix(blocks):
    width = blocks[0].shape[0] - TAIL
    lses = [lse_row(one[width:, :]) for one in blocks]
    top = functools.reduce(jnp.maximum, lses)
    mixes = [jnp.exp(one - top) for one in lses]
    mixed = functools.reduce(jnp.add, mixes)
    inverse = 1.0 / mixed
    total = (mixes[0] * inverse) * blocks[0][:width, :].astype(jnp.float32)
    for one, block in zip(mixes[1:], blocks[1:]):
        total = total + (one * inverse) * block[:width, :].astype(jnp.float32)
    return total, top + jnp.log(mixed)


def near_kernel(*refs):
    out_ref = refs[-1]
    sources, rows, _ = out_ref.shape
    for s in range(sources):
        total, lse = mix([ref[s] for ref in refs[:-1]])
        out_ref[s, : rows - TAIL, :] = total.astype(jnp.bfloat16)
        out_ref[s, rows - TAIL :, :] = tail_rows(lse)


def near_merge(*parts):
    return pl.pallas_call(
        near_kernel,
        in_specs=[VMEM] * len(parts),
        out_specs=VMEM,
        out_shape=jax.ShapeDtypeStruct(parts[0].shape, parts[0].dtype),
        compiler_params=PARAMS,
    )(*parts)


def far_kernel(x_ref, out_ref):
    total, _ = mix([x_ref[s] for s in range(x_ref.shape[0])])
    out_ref[...] = total.T.astype(jnp.bfloat16)


def far_merge(x):
    _, rows, cand = x.shape
    return pl.pallas_call(
        far_kernel,
        in_specs=[VMEM],
        out_specs=VMEM,
        out_shape=jax.ShapeDtypeStruct((cand, rows - TAIL), jnp.bfloat16),
        compiler_params=PARAMS,
    )(x)


def body(chips, queries, hist_keys, hist_values, block_dev, block_local):
    cand, width = queries.shape
    nloc = hist_keys.shape[0] // BLK
    topk = block_dev.shape[1]
    stride = 4
    members = chips // stride

    def shift(x, by):
        pairs = [
            (2 * z + c, 2 * ((z + by(c)) % chips) + c) for z in range(chips) for c in range(2)
        ]
        return lax.ppermute(x, ("z", "core"), pairs)

    far = [[2 * (r + stride * j) + c for j in range(members)] for c in range(2) for r in range(stride)]

    def exchange(x):
        return lax.all_to_all(x, ("z", "core"), 0, 0, tiled=True, axis_index_groups=far)

    swap = [(0, 1), (1, 0)]
    ids = (block_dev * nloc + block_local).astype(jnp.bfloat16).T
    rest = 8
    small = jnp.concatenate([queries[cand - rest :], jnp.pad(ids, ((0, 0), (0, width - cand)))], axis=0)
    xb = lax.all_to_all(
        jnp.broadcast_to(small[None], (chips, rest + topk, width)), "z", 0, 0, tiled=True
    )
    vt = hist_values.T
    keys = (hist_keys, lax.ppermute(hist_keys, "core", swap))
    vts = (vt, lax.ppermute(vt, "core", swap))
    xa = lax.all_gather(queries[: cand - rest], "z")
    z = lax.axis_index("z").astype(jnp.int32)
    core = lax.axis_index("core").astype(jnp.int32)

    def part(by):
        place = [(z + by + chips) % stride, (2 * z + core) * nloc, (2 * z + 1 - core) * nloc]
        return attend(jnp.stack(place), xa, xb, keys, vts, cand, stride)

    steps = (lambda c: 2 - 4 * c, lambda c: 1, lambda c: -1)
    back = [shift(part(by(core)), by) for by in steps]
    merged = near_merge(part(0), *back)
    return far_merge(exchange(merged))


def solution(mesh):
    groups, pos = mesh.devices.shape
    chips = Mesh(mesh.devices.reshape(groups, pos // 2, 2), ("group", "z", "core"))
    spec = P(("group", "z", "core"), None)
    return jax.shard_map(
        functools.partial(body, pos // 2),
        mesh=chips,
        in_specs=(spec,) * 5,
        out_specs=spec,
        check_vma=False,
    )
```

```python
import functools

import jax
import jax.numpy as jnp
from jax import lax
from jax.experimental import pallas as pl
from jax.experimental.pallas import tpu as pltpu
from jax.sharding import Mesh, PartitionSpec as P

BLK = 128
NONE = -1e30
TAIL = 16
VMEM = pl.BlockSpec(memory_space=pltpu.VMEM)
SMEM = pl.BlockSpec(memory_space=pltpu.SMEM)
ANY = pl.BlockSpec(memory_space=pl.ANY)
PARAMS = pltpu.CompilerParams(vmem_limit_bytes=40 * 1024 * 1024)


def tail_rows(lse):
    big = lse.astype(jnp.bfloat16).astype(jnp.float32)
    rest = lse - big
    mid = rest.astype(jnp.bfloat16).astype(jnp.float32)
    row = lax.broadcasted_iota(jnp.int32, (TAIL, lse.shape[1]), 0)
    return jnp.where(row == 0, big, jnp.where(row == 1, mid, rest - mid)).astype(jnp.bfloat16)


def lse_row(tail):
    tail = tail.astype(jnp.float32)
    return tail[0:1] + tail[1:2] + tail[2:3]


def attend_kernel(counts, first_ref, k0_ref, k1_ref, v0_ref, v1_ref, *refs):
    cand = refs[-1].shape[2]
    positions, width = k0_ref.shape
    nloc = positions // BLK
    scale = 1.0 / width**0.5
    slots = [
        (x_ref, out_ref, s)
        for x_ref, out_ref, count in zip(refs, refs[-len(counts) :], counts)
        for s in range(count)
    ]
    for p in range(0, len(slots), 2):
        pair = slots[p : p + 2]
        query = jnp.concatenate([x_ref[s, :cand, :] for x_ref, _, s in pair], axis=0)
        ids = jnp.concatenate(
            [x_ref[s, cand:, :cand].astype(jnp.float32) for x_ref, _, s in pair], axis=1
        )
        parts, lses = [], []
        for half, (k_ref, v_ref) in enumerate(((k0_ref, v0_ref), (k1_ref, v1_ref))):
            near = ids - first_ref[half].astype(jnp.float32)
            inside = jnp.logical_and(near >= 0.0, near < nloc)
            sel = jnp.max(jnp.where(inside, near, -1.0), axis=0, keepdims=True)
            scores = lax.dot_general(
                k_ref[...], query, (((1,), (1,)), ((), ())), preferred_element_type=jnp.float32
            )
            picked = scores[0:BLK]
            for b in range(1, nloc):
                picked = jnp.where(sel == b, scores[b * BLK : (b + 1) * BLK], picked)
            peak = jnp.max(picked, axis=0, keepdims=True)
            expo = jnp.exp((picked - peak) * scale)
            total = jnp.sum(expo, axis=0, keepdims=True)
            spread = jnp.concatenate(
                [jnp.where(sel == b, expo, 0.0).astype(jnp.bfloat16) for b in range(nloc)], axis=0
            )
            summed = jnp.dot(v_ref[...], spread, preferred_element_type=jnp.float32)
            parts.append((summed / total).astype(jnp.bfloat16).astype(jnp.float32))
            lses.append(jnp.where(sel >= 0.0, peak * scale + jnp.log(total), NONE))
        top = jnp.maximum(lses[0], lses[1])
        mix0, mix1 = jnp.exp(lses[0] - top), jnp.exp(lses[1] - top)
        mixed = mix0 + mix1
        merged = ((mix0 / mixed) * parts[0] + (mix1 / mixed) * parts[1]).astype(jnp.bfloat16)
        tail = tail_rows(top + jnp.log(mixed))
        for j, (_, out_ref, s) in enumerate(pair):
            out_ref[s, :width, :] = merged[:, j * cand : (j + 1) * cand]
            out_ref[s, width:, :] = tail[:, j * cand : (j + 1) * cand]


def attend(first, xs, keys, vts, cand, after=()):
    counts = [x.shape[0] for x in xs]
    width = xs[0].shape[2]
    return pl.pallas_call(
        functools.partial(attend_kernel, counts),
        in_specs=[SMEM] + [VMEM] * (4 + len(xs)) + [ANY] * len(after),
        out_specs=[VMEM] * len(xs),
        out_shape=[jax.ShapeDtypeStruct((n, width + TAIL, cand), jnp.bfloat16) for n in counts],
        compiler_params=PARAMS,
    )(first, *keys, *vts, *xs, *after)


def mix(blocks):
    width = blocks[0].shape[0] - TAIL
    lses = [lse_row(one[width:, :]) for one in blocks]
    top = functools.reduce(jnp.maximum, lses)
    mixes = [jnp.exp(one - top) for one in lses]
    mixed = functools.reduce(jnp.add, mixes)
    inverse = 1.0 / mixed
    total = (mixes[0] * inverse) * blocks[0][:width, :].astype(jnp.float32)
    for one, block in zip(mixes[1:], blocks[1:]):
        total = total + (one * inverse) * block[:width, :].astype(jnp.float32)
    return total, top + jnp.log(mixed)


def stack_kernel(*refs):
    out_ref = refs[-1]
    for s in range(out_ref.shape[0]):
        out_ref[s] = refs[s][...]


def stack(blocks, after):
    return pl.pallas_call(
        stack_kernel,
        in_specs=[VMEM] * len(blocks) + [ANY] * len(after),
        out_specs=VMEM,
        out_shape=jax.ShapeDtypeStruct((len(blocks),) + blocks[0].shape, blocks[0].dtype),
        compiler_params=PARAMS,
    )(*blocks, *after)


def near_kernel(*refs):
    *parts, extra, out1_ref, out2_ref = refs
    width = out1_ref.shape[0] - TAIL
    for slot, out_ref in ((1, out1_ref), (2, out2_ref)):
        blocks = [ref[slot] for ref in parts] + ([extra[0]] if slot == 1 else [])
        total, lse = mix(blocks)
        out_ref[:width, :] = total.astype(jnp.bfloat16)
        out_ref[width:, :] = tail_rows(lse)


def near_merge(parts, extra):
    shape = jax.ShapeDtypeStruct(extra.shape[1:], extra.dtype)
    return pl.pallas_call(
        near_kernel,
        in_specs=[VMEM] * (len(parts) + 1),
        out_specs=[VMEM] * 2,
        out_shape=[shape] * 2,
        compiler_params=PARAMS,
    )(*parts, extra)


def far_kernel(*refs):
    *parts, one, two, out_ref = refs
    total, _ = mix([ref[0] for ref in parts] + [one[...], two[...]])
    out_ref[...] = total.T.astype(jnp.bfloat16)


def far_merge(parts, one, two):
    rows, cand = one.shape
    return pl.pallas_call(
        far_kernel,
        in_specs=[VMEM] * (len(parts) + 2),
        out_specs=VMEM,
        out_shape=jax.ShapeDtypeStruct((cand, rows - TAIL), jnp.bfloat16),
        compiler_params=PARAMS,
    )(*parts, one, two)


def body(chips, queries, hist_keys, hist_values, block_dev, block_local):
    cand, width = queries.shape
    nloc = hist_keys.shape[0] // BLK

    def shift(x, by):
        pairs = [
            (2 * z + c, 2 * ((z + by * (1 - 2 * c)) % chips) + c)
            for z in range(chips)
            for c in range(2)
        ]
        return lax.ppermute(x, ("z", "core"), pairs)

    ids = (block_dev * nloc + block_local).astype(jnp.bfloat16).T
    mine = jnp.concatenate([queries, jnp.pad(ids, ((0, 0), (0, width - cand)))], axis=0)
    up5, down5 = shift(mine, -5), shift(mine, 5)

    swap = [(0, 1), (1, 0)]
    vt = hist_values.T
    keys = (hist_keys, lax.ppermute(hist_keys, "core", swap))
    vts = (vt, lax.ppermute(vt, "core", swap))
    here = 2 * lax.axis_index("z").astype(jnp.int32)
    core = lax.axis_index("core").astype(jnp.int32)
    first = jnp.stack([here + core, here + 1 - core]) * nloc

    own = stack([mine, up5, down5], (keys[1], vts[1]))
    up2, down2 = shift(own, -2), shift(own, 2)
    eight = shift(up5[None], -3)
    up1, down1 = shift(own, -1), shift(own, 1)

    part_up2, part_down2 = attend(first, (up2, down2), keys, vts, cand)
    back = [shift(part_up2, 2), shift(part_down2, -2)]
    part_own, part_eight = attend(first, (own, eight), keys, vts, cand, (part_up2,))
    extra = shift(part_eight, 3)
    part_up1, part_down1 = attend(first, (up1, down1), keys, vts, cand, (part_eight,))
    back += [shift(part_up1, 1), shift(part_down1, -1)]
    parts = [part_own] + back
    slot1, slot2 = near_merge(parts, extra)
    return far_merge(parts, shift(slot1, 5), shift(slot2, -5))


def solution(mesh):
    groups, pos = mesh.devices.shape
    chips = Mesh(mesh.devices.reshape(groups, pos // 2, 2), ("group", "z", "core"))
    spec = P(("group", "z", "core"), None)
    return jax.shard_map(
        functools.partial(body, pos // 2),
        mesh=chips,
        in_specs=(spec,) * 5,
        out_specs=spec,
        check_vma=False,
    )
```

```python
import functools

import jax
import jax.numpy as jnp
from jax import lax
from jax.experimental import pallas as pl
from jax.experimental.pallas import tpu as pltpu
from jax.sharding import Mesh, PartitionSpec as P

BLK = 128
NONE = -1e30
TAIL = 16
VMEM = pl.BlockSpec(memory_space=pltpu.VMEM)
SMEM = pl.BlockSpec(memory_space=pltpu.SMEM)
ANY = pl.BlockSpec(memory_space=pl.ANY)
PARAMS = pltpu.CompilerParams(vmem_limit_bytes=40 * 1024 * 1024)


def tail_rows(lse):
    big = lse.astype(jnp.bfloat16).astype(jnp.float32)
    rest = lse - big
    mid = rest.astype(jnp.bfloat16).astype(jnp.float32)
    row = lax.broadcasted_iota(jnp.int32, (TAIL, lse.shape[1]), 0)
    return jnp.where(row == 0, big, jnp.where(row == 1, mid, rest - mid)).astype(jnp.bfloat16)


def lse_row(tail):
    tail = tail.astype(jnp.float32)
    return tail[0:1] + tail[1:2] + tail[2:3]


def attend_kernel(first_ref, x_ref, k0_ref, k1_ref, v0_ref, v1_ref, *refs):
    out_ref = refs[-1]
    sources, _, cand = out_ref.shape
    positions, width = k0_ref.shape
    nloc = positions // BLK
    scale = 1.0 / width**0.5
    for s in range(0, sources, 2):
        query = jnp.concatenate([x_ref[s, :cand, :], x_ref[s + 1, :cand, :]], axis=0)
        ids = jnp.concatenate(
            [
                x_ref[s, cand:, :cand].astype(jnp.float32),
                x_ref[s + 1, cand:, :cand].astype(jnp.float32),
            ],
            axis=1,
        )
        parts, lses = [], []
        for half, (k_ref, v_ref) in enumerate(((k0_ref, v0_ref), (k1_ref, v1_ref))):
            near = ids - first_ref[half].astype(jnp.float32)
            inside = jnp.logical_and(near >= 0.0, near < nloc)
            sel = jnp.max(jnp.where(inside, near, -1.0), axis=0, keepdims=True)
            scores = lax.dot_general(
                k_ref[...], query, (((1,), (1,)), ((), ())), preferred_element_type=jnp.float32
            )
            picked = scores[0:BLK]
            for b in range(1, nloc):
                picked = jnp.where(sel == b, scores[b * BLK : (b + 1) * BLK], picked)
            peak = jnp.max(picked, axis=0, keepdims=True)
            expo = jnp.exp((picked - peak) * scale)
            total = jnp.sum(expo, axis=0, keepdims=True)
            spread = jnp.concatenate(
                [jnp.where(sel == b, expo, 0.0).astype(jnp.bfloat16) for b in range(nloc)], axis=0
            )
            summed = jnp.dot(v_ref[...], spread, preferred_element_type=jnp.float32)
            parts.append((summed / total).astype(jnp.bfloat16).astype(jnp.float32))
            lses.append(jnp.where(sel >= 0.0, peak * scale + jnp.log(total), NONE))
        top = jnp.maximum(lses[0], lses[1])
        mix0, mix1 = jnp.exp(lses[0] - top), jnp.exp(lses[1] - top)
        mixed = mix0 + mix1
        merged = ((mix0 / mixed) * parts[0] + (mix1 / mixed) * parts[1]).astype(jnp.bfloat16)
        tail = tail_rows(top + jnp.log(mixed))
        for j in range(2):
            out_ref[s + j, :width, :] = merged[:, j * cand : (j + 1) * cand]
            out_ref[s + j, width:, :] = tail[:, j * cand : (j + 1) * cand]


def attend(first, x, keys, vts, cand, after=()):
    sources, _, width = x.shape
    return pl.pallas_call(
        attend_kernel,
        in_specs=[SMEM] + [VMEM] * 5 + [ANY] * len(after),
        out_specs=VMEM,
        out_shape=jax.ShapeDtypeStruct((sources, width + TAIL, cand), jnp.bfloat16),
        compiler_params=PARAMS,
    )(first, x, *keys, *vts, *after)


def behind_kernel(x_ref, *refs):
    refs[-1][...] = x_ref[...]


def behind(x, others):
    return pl.pallas_call(
        behind_kernel,
        in_specs=[VMEM] + [ANY] * len(others),
        out_specs=VMEM,
        out_shape=jax.ShapeDtypeStruct(x.shape, x.dtype),
        compiler_params=PARAMS,
    )(x, *others)


def mix(blocks):
    width = blocks[0].shape[0] - TAIL
    lses = [lse_row(one[width:, :]) for one in blocks]
    top = functools.reduce(jnp.maximum, lses)
    mixes = [jnp.exp(one - top) for one in lses]
    mixed = functools.reduce(jnp.add, mixes)
    inverse = 1.0 / mixed
    total = (mixes[0] * inverse) * blocks[0][:width, :].astype(jnp.float32)
    for one, block in zip(mixes[1:], blocks[1:]):
        total = total + (one * inverse) * block[:width, :].astype(jnp.float32)
    return total, top + jnp.log(mixed)


def near_kernel(*refs):
    out_ref = refs[-1]
    sources, rows, _ = out_ref.shape
    for s in range(sources):
        total, lse = mix([ref[s] for ref in refs[:-1]])
        out_ref[s, : rows - TAIL, :] = total.astype(jnp.bfloat16)
        out_ref[s, rows - TAIL :, :] = tail_rows(lse)


def near_merge(*parts):
    return pl.pallas_call(
        near_kernel,
        in_specs=[VMEM] * len(parts),
        out_specs=VMEM,
        out_shape=jax.ShapeDtypeStruct(parts[0].shape, parts[0].dtype),
        compiler_params=PARAMS,
    )(*parts)


def far_kernel(x_ref, out_ref):
    total, _ = mix([x_ref[s] for s in range(x_ref.shape[0])])
    out_ref[...] = total.T.astype(jnp.bfloat16)


def far_merge(x):
    _, rows, cand = x.shape
    return pl.pallas_call(
        far_kernel,
        in_specs=[VMEM],
        out_specs=VMEM,
        out_shape=jax.ShapeDtypeStruct((cand, rows - TAIL), jnp.bfloat16),
        compiler_params=PARAMS,
    )(x)


def body(chips, queries, hist_keys, hist_values, block_dev, block_local):
    cand, width = queries.shape
    nloc = hist_keys.shape[0] // BLK
    topk = block_dev.shape[1]
    stride = 2
    members = chips // stride

    def shift(x, by):
        pairs = [
            (2 * z + c, 2 * ((z + by(c)) % chips) + c) for z in range(chips) for c in range(2)
        ]
        return lax.ppermute(x, ("z", "core"), pairs)

    far = [[2 * (r + stride * j) + c for j in range(members)] for c in range(2) for r in range(stride)]

    def exchange(x):
        return lax.all_to_all(x, ("z", "core"), 0, 0, tiled=True, axis_index_groups=far)

    swap = [(0, 1), (1, 0)]
    ids = (block_dev * nloc + block_local).astype(jnp.bfloat16).T
    mine = jnp.concatenate([queries, jnp.pad(ids, ((0, 0), (0, width - cand)))], axis=0)
    own = exchange(jnp.broadcast_to(mine[None], (members, cand + topk, width)))
    vt = hist_values.T
    keys = (hist_keys, lax.ppermute(hist_keys, "core", swap))
    vts = (vt, lax.ppermute(vt, "core", swap))
    here = 2 * lax.axis_index("z").astype(jnp.int32)
    core = lax.axis_index("core").astype(jnp.int32)
    first = jnp.stack([here + core, here + 1 - core]) * nloc

    own = behind(own, (keys[1], vts[1]))
    other = shift(own, lambda c: 1 - 2 * c)
    own_part = attend(first, own, keys, vts, cand)
    other_part = attend(first, other, keys, vts, cand, (own_part,))
    merged = near_merge(own_part, shift(other_part, lambda c: 2 * c - 1))
    return far_merge(exchange(merged))


def solution(mesh):
    groups, pos = mesh.devices.shape
    chips = Mesh(mesh.devices.reshape(groups, pos // 2, 2), ("group", "z", "core"))
    spec = P(("group", "z", "core"), None)
    return jax.shard_map(
        functools.partial(body, pos // 2),
        mesh=chips,
        in_specs=(spec,) * 5,
        out_specs=spec,
        check_vma=False,
    )
```

```python
import functools

import jax
import jax.numpy as jnp
from jax import lax
from jax.experimental import pallas as pl
from jax.experimental.pallas import tpu as pltpu
from jax.sharding import Mesh, PartitionSpec as P

BLK = 128
NONE = -1e30
TAIL = 16
VMEM = pl.BlockSpec(memory_space=pltpu.VMEM)
SMEM = pl.BlockSpec(memory_space=pltpu.SMEM)
PARAMS = pltpu.CompilerParams(vmem_limit_bytes=20 * 1024 * 1024)


def tail_rows(lse):
    big = lse.astype(jnp.bfloat16).astype(jnp.float32)
    rest = lse - big
    mid = rest.astype(jnp.bfloat16).astype(jnp.float32)
    row = lax.broadcasted_iota(jnp.int32, (TAIL, lse.shape[1]), 0)
    return jnp.where(row == 0, big, jnp.where(row == 1, mid, rest - mid)).astype(jnp.bfloat16)


def lse_row(tail):
    tail = tail.astype(jnp.float32)
    return tail[0:1] + tail[1:2] + tail[2:3]


def attend_kernel(stride, place_ref, xa_ref, xb_ref, k_ref, v_ref, out_ref):
    members, _, cand = out_ref.shape
    rest = cand - xa_ref.shape[1]
    _, positions, width = k_ref.shape
    nloc = positions // BLK
    scale = 1.0 / width**0.5
    def pair(p, carry):
        s = 2 * p
        rows, ids = [], []
        for j in range(2):
            source = place_ref[0] + stride * (s + j)
            small = xb_ref[source]
            rows += [xa_ref[source], small[:rest]]
            ids.append(small[rest:, :cand].astype(jnp.float32))
        query = jnp.concatenate(rows, axis=0)
        ids = jnp.concatenate(ids, axis=1)
        parts, lses = [], []
        for half in range(2):
            near = ids - (place_ref[1] + half * nloc).astype(jnp.float32)
            inside = jnp.logical_and(near >= 0.0, near < nloc)
            sel = jnp.max(jnp.where(inside, near, -1.0), axis=0, keepdims=True)
            scores = lax.dot_general(
                k_ref[half], query, (((1,), (1,)), ((), ())), preferred_element_type=jnp.float32
            )
            picked = scores[0:BLK]
            for b in range(1, nloc):
                picked = jnp.where(sel == b, scores[b * BLK : (b + 1) * BLK], picked)
            peak = jnp.max(picked, axis=0, keepdims=True)
            expo = jnp.exp((picked - peak) * scale)
            total = jnp.sum(expo, axis=0, keepdims=True)
            spread = jnp.concatenate(
                [jnp.where(sel == b, expo, 0.0).astype(jnp.bfloat16) for b in range(nloc)], axis=0
            )
            summed = jnp.dot(v_ref[half], spread, preferred_element_type=jnp.float32)
            parts.append((summed / total).astype(jnp.bfloat16).astype(jnp.float32))
            lses.append(jnp.where(sel >= 0.0, peak * scale + jnp.log(total), NONE))
        top = jnp.maximum(lses[0], lses[1])
        mix0, mix1 = jnp.exp(lses[0] - top), jnp.exp(lses[1] - top)
        mixed = mix0 + mix1
        merged = ((mix0 / mixed) * parts[0] + (mix1 / mixed) * parts[1]).astype(jnp.bfloat16)
        tail = tail_rows(top + jnp.log(mixed))
        for j in range(2):
            out_ref[s + j, :width, :] = merged[:, j * cand : (j + 1) * cand]
            out_ref[s + j, width:, :] = tail[:, j * cand : (j + 1) * cand]
        return carry

    lax.fori_loop(0, members // 2, pair, 0)


def attend(place, xa, xb, keys, vts, cand, stride):
    chips, _, width = xa.shape
    return pl.pallas_call(
        functools.partial(attend_kernel, stride),
        in_specs=[SMEM] + [VMEM] * 4,
        out_specs=VMEM,
        out_shape=jax.ShapeDtypeStruct((chips // stride, width + TAIL, cand), jnp.bfloat16),
        compiler_params=PARAMS,
    )(place, xa, xb, keys, vts)


def mix(blocks):
    width = blocks[0].shape[0] - TAIL
    lses = [lse_row(one[width:, :]) for one in blocks]
    top = functools.reduce(jnp.maximum, lses)
    mixes = [jnp.exp(one - top) for one in lses]
    mixed = functools.reduce(jnp.add, mixes)
    inverse = 1.0 / mixed
    total = (mixes[0] * inverse) * blocks[0][:width, :].astype(jnp.float32)
    for one, block in zip(mixes[1:], blocks[1:]):
        total = total + (one * inverse) * block[:width, :].astype(jnp.float32)
    return total, top + jnp.log(mixed)


def near_kernel(*refs):
    out_ref = refs[-1]
    sources, rows, _ = out_ref.shape
    for s in range(sources):
        total, lse = mix([ref[s] for ref in refs[:-1]])
        out_ref[s, : rows - TAIL, :] = total.astype(jnp.bfloat16)
        out_ref[s, rows - TAIL :, :] = tail_rows(lse)


def near_merge(*parts):
    return pl.pallas_call(
        near_kernel,
        in_specs=[VMEM] * len(parts),
        out_specs=VMEM,
        out_shape=jax.ShapeDtypeStruct(parts[0].shape, parts[0].dtype),
        compiler_params=PARAMS,
    )(*parts)


def far_kernel(x_ref, out_ref):
    total, _ = mix([x_ref[s] for s in range(x_ref.shape[0])])
    out_ref[...] = total.T.astype(jnp.bfloat16)


def far_merge(x):
    _, rows, cand = x.shape
    return pl.pallas_call(
        far_kernel,
        in_specs=[VMEM],
        out_specs=VMEM,
        out_shape=jax.ShapeDtypeStruct((cand, rows - TAIL), jnp.bfloat16),
        compiler_params=PARAMS,
    )(x)


def body(chips, queries, hist_keys, hist_values, block_dev, block_local):
    cand, width = queries.shape
    nloc = hist_keys.shape[0] // BLK
    topk = block_dev.shape[1]
    stride = 4
    members = chips // stride

    def shift(x, by):
        pairs = [
            (2 * z + c, 2 * ((z + by(c)) % chips) + c) for z in range(chips) for c in range(2)
        ]
        return lax.ppermute(x, ("z", "core"), pairs)

    far = [[2 * (r + stride * j) + c for j in range(members)] for c in range(2) for r in range(stride)]

    def exchange(x):
        return lax.all_to_all(x, ("z", "core"), 0, 0, tiled=True, axis_index_groups=far)

    keys = lax.all_gather(hist_keys, "core")
    vts = lax.all_gather(hist_values.T, "core")
    ids = (block_dev * nloc + block_local).astype(jnp.bfloat16).T
    rest = cand // 4
    small = jnp.concatenate([queries[cand - rest :], jnp.pad(ids, ((0, 0), (0, width - cand)))], axis=0)
    xb = lax.all_to_all(
        jnp.broadcast_to(small[None], (chips, rest + topk, width)), "z", 0, 0, tiled=True
    )
    xa = lax.all_gather(queries[: cand - rest], "z")
    z = lax.axis_index("z").astype(jnp.int32)
    core = lax.axis_index("core").astype(jnp.int32)

    def part(by):
        place = [(z + by + chips) % stride, 2 * z * nloc]
        return attend(jnp.stack(place), xa, xb, keys, vts, cand, stride)

    steps = (lambda c: 2 - 4 * c, lambda c: 1, lambda c: -1)
    back = [shift(part(by(core)), by) for by in steps]
    merged = near_merge(part(0), *back)
    return far_merge(exchange(merged))


def solution(mesh):
    groups, pos = mesh.devices.shape
    chips = Mesh(mesh.devices.reshape(groups, pos // 2, 2), ("group", "z", "core"))
    spec = P(("group", "z", "core"), None)
    return jax.shard_map(
        functools.partial(body, pos // 2),
        mesh=chips,
        in_specs=(spec,) * 5,
        out_specs=spec,
        check_vma=False,
    )
```

```python
import functools

import jax
import jax.numpy as jnp
from jax import lax
from jax.experimental import pallas as pl
from jax.experimental.pallas import tpu as pltpu
from jax.sharding import Mesh, PartitionSpec as P

BLK = 128
NONE = -1e30
TAIL = 16
VMEM = pl.BlockSpec(memory_space=pltpu.VMEM)
SMEM = pl.BlockSpec(memory_space=pltpu.SMEM)
ANY = pl.BlockSpec(memory_space=pl.ANY)
PARAMS = pltpu.CompilerParams(vmem_limit_bytes=40 * 1024 * 1024)


def tail_rows(lse):
    big = lse.astype(jnp.bfloat16).astype(jnp.float32)
    rest = lse - big
    mid = rest.astype(jnp.bfloat16).astype(jnp.float32)
    row = lax.broadcasted_iota(jnp.int32, (TAIL, lse.shape[1]), 0)
    return jnp.where(row == 0, big, jnp.where(row == 1, mid, rest - mid)).astype(jnp.bfloat16)


def lse_row(tail):
    tail = tail.astype(jnp.float32)
    return tail[0:1] + tail[1:2] + tail[2:3]


def attend_kernel(counts, first_ref, k0_ref, k1_ref, v0_ref, v1_ref, *refs):
    cand = refs[-1].shape[2]
    positions, width = k0_ref.shape
    nloc = positions // BLK
    scale = 1.0 / width**0.5
    slots = [
        (x_ref, out_ref, s)
        for x_ref, out_ref, count in zip(refs, refs[-len(counts) :], counts)
        for s in range(count)
    ]
    for p in range(0, len(slots), 2):
        pair = slots[p : p + 2]
        query = jnp.concatenate([x_ref[s, :cand, :] for x_ref, _, s in pair], axis=0)
        ids = jnp.concatenate(
            [x_ref[s, cand:, :cand].astype(jnp.float32) for x_ref, _, s in pair], axis=1
        )
        parts, lses = [], []
        for half, (k_ref, v_ref) in enumerate(((k0_ref, v0_ref), (k1_ref, v1_ref))):
            near = ids - first_ref[half].astype(jnp.float32)
            inside = jnp.logical_and(near >= 0.0, near < nloc)
            sel = jnp.max(jnp.where(inside, near, -1.0), axis=0, keepdims=True)
            scores = lax.dot_general(
                k_ref[...], query, (((1,), (1,)), ((), ())), preferred_element_type=jnp.float32
            )
            picked = scores[0:BLK]
            for b in range(1, nloc):
                picked = jnp.where(sel == b, scores[b * BLK : (b + 1) * BLK], picked)
            peak = jnp.max(picked, axis=0, keepdims=True)
            expo = jnp.exp((picked - peak) * scale)
            total = jnp.sum(expo, axis=0, keepdims=True)
            spread = jnp.concatenate(
                [jnp.where(sel == b, expo, 0.0).astype(jnp.bfloat16) for b in range(nloc)], axis=0
            )
            summed = jnp.dot(v_ref[...], spread, preferred_element_type=jnp.float32)
            parts.append((summed / total).astype(jnp.bfloat16).astype(jnp.float32))
            lses.append(jnp.where(sel >= 0.0, peak * scale + jnp.log(total), NONE))
        top = jnp.maximum(lses[0], lses[1])
        mix0, mix1 = jnp.exp(lses[0] - top), jnp.exp(lses[1] - top)
        mixed = mix0 + mix1
        merged = ((mix0 / mixed) * parts[0] + (mix1 / mixed) * parts[1]).astype(jnp.bfloat16)
        tail = tail_rows(top + jnp.log(mixed))
        for j, (_, out_ref, s) in enumerate(pair):
            out_ref[s, :width, :] = merged[:, j * cand : (j + 1) * cand]
            out_ref[s, width:, :] = tail[:, j * cand : (j + 1) * cand]


def attend(first, xs, keys, vts, cand, after=()):
    counts = [x.shape[0] for x in xs]
    width = xs[0].shape[2]
    return pl.pallas_call(
        functools.partial(attend_kernel, counts),
        in_specs=[SMEM] + [VMEM] * (4 + len(xs)) + [ANY] * len(after),
        out_specs=[VMEM] * len(xs),
        out_shape=[jax.ShapeDtypeStruct((n, width + TAIL, cand), jnp.bfloat16) for n in counts],
        compiler_params=PARAMS,
    )(first, *keys, *vts, *xs, *after)


def halves_kernel(x_ref, *refs):
    low_ref, high_ref = refs[-2:]
    half = low_ref.shape[0]
    low_ref[...] = x_ref[:half]
    high_ref[...] = x_ref[half:]


def halves(x, others):
    shape = jax.ShapeDtypeStruct((x.shape[0] // 2,) + x.shape[1:], x.dtype)
    return pl.pallas_call(
        halves_kernel,
        in_specs=[VMEM] + [ANY] * len(others),
        out_specs=[VMEM] * 2,
        out_shape=[shape] * 2,
        compiler_params=PARAMS,
    )(x, *others)


def mix(blocks):
    width = blocks[0].shape[0] - TAIL
    lses = [lse_row(one[width:, :]) for one in blocks]
    top = functools.reduce(jnp.maximum, lses)
    mixes = [jnp.exp(one - top) for one in lses]
    mixed = functools.reduce(jnp.add, mixes)
    inverse = 1.0 / mixed
    total = (mixes[0] * inverse) * blocks[0][:width, :].astype(jnp.float32)
    for one, block in zip(mixes[1:], blocks[1:]):
        total = total + (one * inverse) * block[:width, :].astype(jnp.float32)
    return total, top + jnp.log(mixed)


def near_kernel(low0_ref, high0_ref, low1_ref, high1_ref, out_ref):
    half, rows, _ = low0_ref.shape
    for s in range(out_ref.shape[0]):
        refs = (low0_ref, low1_ref) if s < half else (high0_ref, high1_ref)
        total, lse = mix([ref[s % half] for ref in refs])
        out_ref[s, : rows - TAIL, :] = total.astype(jnp.bfloat16)
        out_ref[s, rows - TAIL :, :] = tail_rows(lse)


def near_merge(own, other):
    half, rows, cand = own[0].shape
    return pl.pallas_call(
        near_kernel,
        in_specs=[VMEM] * 4,
        out_specs=VMEM,
        out_shape=jax.ShapeDtypeStruct((2 * half, rows, cand), own[0].dtype),
        compiler_params=PARAMS,
    )(*own, *other)


def far_kernel(x_ref, out_ref):
    total, _ = mix([x_ref[s] for s in range(x_ref.shape[0])])
    out_ref[...] = total.T.astype(jnp.bfloat16)


def far_merge(x):
    _, rows, cand = x.shape
    return pl.pallas_call(
        far_kernel,
        in_specs=[VMEM],
        out_specs=VMEM,
        out_shape=jax.ShapeDtypeStruct((cand, rows - TAIL), jnp.bfloat16),
        compiler_params=PARAMS,
    )(x)


def body(chips, queries, hist_keys, hist_values, block_dev, block_local):
    cand, width = queries.shape
    nloc = hist_keys.shape[0] // BLK
    topk = block_dev.shape[1]
    group = [0, 1, 3, 5, 7, 10, 12, 14]
    groups = [group, [z for z in range(chips) if z not in group]]
    far = [[2 * ((z + c) % chips) + c for z in one] for c in range(2) for one in groups]

    def partner(x):
        pairs = [
            (2 * z + c, 2 * ((z + (1 if (z + c) % 2 else -1)) % chips) + c)
            for z in range(chips)
            for c in range(2)
        ]
        return lax.ppermute(x, ("z", "core"), pairs)

    def exchange(x):
        return lax.all_to_all(x, ("z", "core"), 0, 0, tiled=True, axis_index_groups=far)

    swap = [(0, 1), (1, 0)]
    ids = (block_dev * nloc + block_local).astype(jnp.bfloat16).T
    mine = jnp.concatenate([queries, jnp.pad(ids, ((0, 0), (0, width - cand)))], axis=0)
    own = exchange(jnp.broadcast_to(mine[None], (len(group), cand + topk, width)))
    vt = hist_values.T
    keys = (hist_keys, lax.ppermute(hist_keys, "core", swap))
    vts = (vt, lax.ppermute(vt, "core", swap))
    here = 2 * lax.axis_index("z").astype(jnp.int32)
    core = lax.axis_index("core").astype(jnp.int32)
    first = jnp.stack([here + core, here + 1 - core]) * nloc

    own = halves(own, (keys[1], vts[1]))
    other = [partner(x) for x in own]
    back = [partner(attend(first, (x,), keys, vts, cand)[0]) for x in other]
    merged = near_merge(attend(first, own, keys, vts, cand), back)
    return far_merge(exchange(merged))


def solution(mesh):
    groups, pos = mesh.devices.shape
    chips = Mesh(mesh.devices.reshape(groups, pos // 2, 2), ("group", "z", "core"))
    spec = P(("group", "z", "core"), None)
    return jax.shard_map(
        functools.partial(body, pos // 2),
        mesh=chips,
        in_specs=(spec,) * 5,
        out_specs=spec,
        check_vma=False,
    )
```

```python
import functools

import jax
import jax.numpy as jnp
from jax import lax
from jax.experimental import pallas as pl
from jax.experimental.pallas import tpu as pltpu
from jax.sharding import Mesh, PartitionSpec as P

BLK = 128
NONE = -1e30
TAIL = 16
VMEM = pl.BlockSpec(memory_space=pltpu.VMEM)
SMEM = pl.BlockSpec(memory_space=pltpu.SMEM)
ANY = pl.BlockSpec(memory_space=pl.ANY)
PARAMS = pltpu.CompilerParams(vmem_limit_bytes=40 * 1024 * 1024)


def tail_rows(lse):
    big = lse.astype(jnp.bfloat16).astype(jnp.float32)
    rest = lse - big
    mid = rest.astype(jnp.bfloat16).astype(jnp.float32)
    row = lax.broadcasted_iota(jnp.int32, (TAIL, lse.shape[1]), 0)
    return jnp.where(row == 0, big, jnp.where(row == 1, mid, rest - mid)).astype(jnp.bfloat16)


def lse_row(tail):
    tail = tail.astype(jnp.float32)
    return tail[0:1] + tail[1:2] + tail[2:3]


def attend_kernel(counts, first_ref, k0_ref, k1_ref, v0_ref, v1_ref, *refs):
    cand = refs[-1].shape[2]
    positions, width = k0_ref.shape
    nloc = positions // BLK
    scale = 1.0 / width**0.5
    slots = [
        (x_ref, out_ref, s)
        for x_ref, out_ref, count in zip(refs, refs[-len(counts) :], counts)
        for s in range(count)
    ]
    for p in range(0, len(slots), 2):
        pair = slots[p : p + 2]
        query = jnp.concatenate([x_ref[s, :cand, :] for x_ref, _, s in pair], axis=0)
        ids = jnp.concatenate(
            [x_ref[s, cand:, :cand].astype(jnp.float32) for x_ref, _, s in pair], axis=1
        )
        parts, lses = [], []
        for half, (k_ref, v_ref) in enumerate(((k0_ref, v0_ref), (k1_ref, v1_ref))):
            near = ids - first_ref[half].astype(jnp.float32)
            inside = jnp.logical_and(near >= 0.0, near < nloc)
            sel = jnp.max(jnp.where(inside, near, -1.0), axis=0, keepdims=True)
            scores = lax.dot_general(
                k_ref[...], query, (((1,), (1,)), ((), ())), preferred_element_type=jnp.float32
            )
            picked = scores[0:BLK]
            for b in range(1, nloc):
                picked = jnp.where(sel == b, scores[b * BLK : (b + 1) * BLK], picked)
            peak = jnp.max(picked, axis=0, keepdims=True)
            expo = jnp.exp((picked - peak) * scale)
            total = jnp.sum(expo, axis=0, keepdims=True)
            spread = jnp.concatenate(
                [jnp.where(sel == b, expo, 0.0).astype(jnp.bfloat16) for b in range(nloc)], axis=0
            )
            summed = jnp.dot(v_ref[...], spread, preferred_element_type=jnp.float32)
            parts.append((summed / total).astype(jnp.bfloat16).astype(jnp.float32))
            lses.append(jnp.where(sel >= 0.0, peak * scale + jnp.log(total), NONE))
        top = jnp.maximum(lses[0], lses[1])
        mix0, mix1 = jnp.exp(lses[0] - top), jnp.exp(lses[1] - top)
        mixed = mix0 + mix1
        merged = ((mix0 / mixed) * parts[0] + (mix1 / mixed) * parts[1]).astype(jnp.bfloat16)
        tail = tail_rows(top + jnp.log(mixed))
        for j, (_, out_ref, s) in enumerate(pair):
            out_ref[s, :width, :] = merged[:, j * cand : (j + 1) * cand]
            out_ref[s, width:, :] = tail[:, j * cand : (j + 1) * cand]


def attend(first, xs, keys, vts, cand, after=()):
    counts = [x.shape[0] for x in xs]
    width = xs[0].shape[2]
    return pl.pallas_call(
        functools.partial(attend_kernel, counts),
        in_specs=[SMEM] + [VMEM] * (4 + len(xs)) + [ANY] * len(after),
        out_specs=[VMEM] * len(xs),
        out_shape=[jax.ShapeDtypeStruct((n, width + TAIL, cand), jnp.bfloat16) for n in counts],
        compiler_params=PARAMS,
    )(first, *keys, *vts, *xs, *after)


def mix(blocks):
    width = blocks[0].shape[0] - TAIL
    lses = [lse_row(one[width:, :]) for one in blocks]
    top = functools.reduce(jnp.maximum, lses)
    mixes = [jnp.exp(one - top) for one in lses]
    mixed = functools.reduce(jnp.add, mixes)
    inverse = 1.0 / mixed
    total = (mixes[0] * inverse) * blocks[0][:width, :].astype(jnp.float32)
    for one, block in zip(mixes[1:], blocks[1:]):
        total = total + (one * inverse) * block[:width, :].astype(jnp.float32)
    return total, top + jnp.log(mixed)


def near_kernel(*refs):
    *parts, extra, out1_ref, out2_ref = refs
    width = out1_ref.shape[0] - TAIL
    for slot, out_ref in ((1, out1_ref), (2, out2_ref)):
        blocks = [ref[slot] for ref in parts] + ([extra[0]] if slot == 1 else [])
        total, lse = mix(blocks)
        out_ref[:width, :] = total.astype(jnp.bfloat16)
        out_ref[width:, :] = tail_rows(lse)


def near_merge(parts, extra):
    shape = jax.ShapeDtypeStruct(extra.shape[1:], extra.dtype)
    return pl.pallas_call(
        near_kernel,
        in_specs=[VMEM] * (len(parts) + 1),
        out_specs=[VMEM] * 2,
        out_shape=[shape] * 2,
        compiler_params=PARAMS,
    )(*parts, extra)


def far_kernel(*refs):
    *parts, one, two, out_ref = refs
    total, _ = mix([ref[0] for ref in parts] + [one[...], two[...]])
    out_ref[...] = total.T.astype(jnp.bfloat16)


def far_merge(parts, one, two):
    rows, cand = one.shape
    return pl.pallas_call(
        far_kernel,
        in_specs=[VMEM] * (len(parts) + 2),
        out_specs=VMEM,
        out_shape=jax.ShapeDtypeStruct((cand, rows - TAIL), jnp.bfloat16),
        compiler_params=PARAMS,
    )(*parts, one, two)


def body(chips, queries, hist_keys, hist_values, block_dev, block_local):
    cand, width = queries.shape
    nloc = hist_keys.shape[0] // BLK

    def shift(x, by):
        pairs = [
            (2 * z + c, 2 * ((z + by * (1 - 2 * c)) % chips) + c)
            for z in range(chips)
            for c in range(2)
        ]
        return lax.ppermute(x, ("z", "core"), pairs)

    ids = (block_dev * nloc + block_local).astype(jnp.bfloat16).T
    mine = jnp.concatenate([queries, jnp.pad(ids, ((0, 0), (0, width - cand)))], axis=0)
    up5, down5 = shift(mine, -5), shift(mine, 5)

    swap = [(0, 1), (1, 0)]
    vt = hist_values.T
    keys = (hist_keys, lax.ppermute(hist_keys, "core", swap))
    vts = (vt, lax.ppermute(vt, "core", swap))
    here = 2 * lax.axis_index("z").astype(jnp.int32)
    core = lax.axis_index("core").astype(jnp.int32)
    first = jnp.stack([here + core, here + 1 - core]) * nloc

    own = jnp.stack([mine, up5, down5])
    up2, down2 = shift(own, -2), shift(own, 2)
    eight = shift(up5[None], -3)
    up1, down1 = shift(own, -1), shift(own, 1)

    part_up2, part_down2 = attend(first, (up2, down2), keys, vts, cand)
    back = [shift(part_up2, 2), shift(part_down2, -2)]
    part_own, part_eight = attend(first, (own, eight), keys, vts, cand, (part_up2,))
    extra = shift(part_eight, 3)
    part_up1, part_down1 = attend(first, (up1, down1), keys, vts, cand, (part_eight,))
    back += [shift(part_up1, 1), shift(part_down1, -1)]
    parts = [part_own] + back
    slot1, slot2 = near_merge(parts, extra)
    return far_merge(parts, shift(slot1, 5), shift(slot2, -5))


def solution(mesh):
    groups, pos = mesh.devices.shape
    chips = Mesh(mesh.devices.reshape(groups, pos // 2, 2), ("group", "z", "core"))
    spec = P(("group", "z", "core"), None)
    return jax.shard_map(
        functools.partial(body, pos // 2),
        mesh=chips,
        in_specs=(spec,) * 5,
        out_specs=spec,
        check_vma=False,
    )
```

```python
import functools

import jax
import jax.numpy as jnp
from jax import lax
from jax.experimental import pallas as pl
from jax.experimental.pallas import tpu as pltpu
from jax.sharding import Mesh, PartitionSpec as P

BLK = 128
NONE = -1e30
TAIL = 16
VMEM = pl.BlockSpec(memory_space=pltpu.VMEM)
SMEM = pl.BlockSpec(memory_space=pltpu.SMEM)
PARAMS = pltpu.CompilerParams(vmem_limit_bytes=40 * 1024 * 1024)


def tail_rows(lse):
    big = lse.astype(jnp.bfloat16).astype(jnp.float32)
    rest = lse - big
    mid = rest.astype(jnp.bfloat16).astype(jnp.float32)
    row = lax.broadcasted_iota(jnp.int32, (TAIL, lse.shape[1]), 0)
    return jnp.where(row == 0, big, jnp.where(row == 1, mid, rest - mid)).astype(jnp.bfloat16)


def lse_row(tail):
    tail = tail.astype(jnp.float32)
    return tail[0:1] + tail[1:2] + tail[2:3]


def attend_kernel(place_ref, x_ref, k0_ref, k1_ref, v0_ref, v1_ref, out_ref):
    sources, _, cand = out_ref.shape
    positions, width = k0_ref.shape
    nloc = positions // BLK
    scale = 1.0 / width**0.5
    for s in range(0, sources, 2):
        one, two = place_ref[0] + s, place_ref[0] + s + 1
        query = jnp.concatenate([x_ref[one, :cand, :], x_ref[two, :cand, :]], axis=0)
        ids = jnp.concatenate(
            [
                x_ref[one, cand:, :cand].astype(jnp.float32),
                x_ref[two, cand:, :cand].astype(jnp.float32),
            ],
            axis=1,
        )
        parts, lses = [], []
        for half, (k_ref, v_ref) in enumerate(((k0_ref, v0_ref), (k1_ref, v1_ref))):
            near = ids - place_ref[1 + half].astype(jnp.float32)
            inside = jnp.logical_and(near >= 0.0, near < nloc)
            sel = jnp.max(jnp.where(inside, near, -1.0), axis=0, keepdims=True)
            scores = lax.dot_general(
                k_ref[...], query, (((1,), (1,)), ((), ())), preferred_element_type=jnp.float32
            )
            picked = scores[0:BLK]
            for b in range(1, nloc):
                picked = jnp.where(sel == b, scores[b * BLK : (b + 1) * BLK], picked)
            peak = jnp.max(picked, axis=0, keepdims=True)
            expo = jnp.exp((picked - peak) * scale)
            total = jnp.sum(expo, axis=0, keepdims=True)
            spread = jnp.concatenate(
                [jnp.where(sel == b, expo, 0.0).astype(jnp.bfloat16) for b in range(nloc)], axis=0
            )
            summed = jnp.dot(v_ref[...], spread, preferred_element_type=jnp.float32)
            parts.append((summed / total).astype(jnp.bfloat16).astype(jnp.float32))
            lses.append(jnp.where(sel >= 0.0, peak * scale + jnp.log(total), NONE))
        top = jnp.maximum(lses[0], lses[1])
        mix0, mix1 = jnp.exp(lses[0] - top), jnp.exp(lses[1] - top)
        mixed = mix0 + mix1
        merged = ((mix0 / mixed) * parts[0] + (mix1 / mixed) * parts[1]).astype(jnp.bfloat16)
        tail = tail_rows(top + jnp.log(mixed))
        for j in range(2):
            out_ref[s + j, :width, :] = merged[:, j * cand : (j + 1) * cand]
            out_ref[s + j, width:, :] = tail[:, j * cand : (j + 1) * cand]


def attend(place, x, keys, vts, cand, sources):
    width = x.shape[2]
    return pl.pallas_call(
        attend_kernel,
        in_specs=[SMEM] + [VMEM] * 5,
        out_specs=VMEM,
        out_shape=jax.ShapeDtypeStruct((sources, width + TAIL, cand), jnp.bfloat16),
        compiler_params=PARAMS,
    )(jnp.stack(place), x, *keys, *vts)


def mix(blocks):
    width = blocks[0].shape[0] - TAIL
    lses = [lse_row(one[width:, :]) for one in blocks]
    top = functools.reduce(jnp.maximum, lses)
    mixes = [jnp.exp(one - top) for one in lses]
    mixed = functools.reduce(jnp.add, mixes)
    inverse = 1.0 / mixed
    total = (mixes[0] * inverse) * blocks[0][:width, :].astype(jnp.float32)
    for one, block in zip(mixes[1:], blocks[1:]):
        total = total + (one * inverse) * block[:width, :].astype(jnp.float32)
    return total, top + jnp.log(mixed)


def near_kernel(*refs):
    out_ref = refs[-1]
    sources, rows, _ = out_ref.shape
    for s in range(sources):
        total, lse = mix([ref[s] for ref in refs[:-1]])
        out_ref[s, : rows - TAIL, :] = total.astype(jnp.bfloat16)
        out_ref[s, rows - TAIL :, :] = tail_rows(lse)


def near_merge(*parts):
    return pl.pallas_call(
        near_kernel,
        in_specs=[VMEM] * len(parts),
        out_specs=VMEM,
        out_shape=jax.ShapeDtypeStruct(parts[0].shape, parts[0].dtype),
        compiler_params=PARAMS,
    )(*parts)


def far_kernel(x_ref, out_ref):
    total, _ = mix([x_ref[s] for s in range(x_ref.shape[0])])
    out_ref[...] = total.T.astype(jnp.bfloat16)


def far_merge(x):
    _, rows, cand = x.shape
    return pl.pallas_call(
        far_kernel,
        in_specs=[VMEM],
        out_specs=VMEM,
        out_shape=jax.ShapeDtypeStruct((cand, rows - TAIL), jnp.bfloat16),
        compiler_params=PARAMS,
    )(x)


def body(chips, queries, hist_keys, hist_values, block_dev, block_local):
    cand, width = queries.shape
    nloc = hist_keys.shape[0] // BLK
    topk = block_dev.shape[1]
    stride = 4
    members = chips // stride

    def shift(x, by):
        pairs = [
            (2 * z + c, 2 * ((z + by(c)) % chips) + c) for z in range(chips) for c in range(2)
        ]
        return lax.ppermute(x, ("z", "core"), pairs)

    far = [[2 * (r + stride * j) + c for j in range(members)] for c in range(2) for r in range(stride)]

    near = [
        [2 * ((stride * i + 2 * c + j) % chips) + c for j in range(stride)]
        for c in range(2)
        for i in range(members)
    ]

    def exchange(x, groups):
        return lax.all_to_all(x, ("z", "core"), 0, 0, tiled=True, axis_index_groups=groups)

    swap = [(0, 1), (1, 0)]
    ids = (block_dev * nloc + block_local).astype(jnp.bfloat16).T
    mine = jnp.concatenate([queries, jnp.pad(ids, ((0, 0), (0, width - cand)))], axis=0)
    own = exchange(jnp.broadcast_to(mine[None], (members, cand + topk, width)), far)
    vt = hist_values.T
    keys = (hist_keys, lax.ppermute(hist_keys, "core", swap))
    vts = (vt, lax.ppermute(vt, "core", swap))
    z = lax.axis_index("z").astype(jnp.int32)
    core = lax.axis_index("core").astype(jnp.int32)
    halves = [(2 * z + core) * nloc, (2 * z + 1 - core) * nloc]
    every = exchange(jnp.broadcast_to(own[None], (stride,) + own.shape), near)
    every = every.reshape((stride * members,) + own.shape[1:])

    def part(by):
        line = (z + by - 2 * core + 2 * stride) % stride
        return attend([line * members] + halves, every, keys, vts, cand, members)

    mine_part = attend([jnp.int32(0)] + halves, own, keys, vts, cand, members)
    steps = (lambda c: 2 - 4 * c, lambda c: 1, lambda c: -1)
    back = [shift(part(by(core)), by) for by in steps]
    merged = near_merge(mine_part, *back)
    return far_merge(exchange(merged, far))


def solution(mesh):
    groups, pos = mesh.devices.shape
    chips = Mesh(mesh.devices.reshape(groups, pos // 2, 2), ("group", "z", "core"))
    spec = P(("group", "z", "core"), None)
    return jax.shard_map(
        functools.partial(body, pos // 2),
        mesh=chips,
        in_specs=(spec,) * 5,
        out_specs=spec,
        check_vma=False,
    )
```

```python
import functools

import jax
import jax.numpy as jnp
from jax import lax
from jax.experimental import pallas as pl
from jax.experimental.pallas import tpu as pltpu
from jax.sharding import Mesh, PartitionSpec as P

BLK = 128
NONE = -1e30
TAIL = 16
VMEM = pl.BlockSpec(memory_space=pltpu.VMEM)
SMEM = pl.BlockSpec(memory_space=pltpu.SMEM)
ANY = pl.BlockSpec(memory_space=pl.ANY)
PARAMS = pltpu.CompilerParams(vmem_limit_bytes=40 * 1024 * 1024)


def tail_rows(lse):
    big = lse.astype(jnp.bfloat16).astype(jnp.float32)
    rest = lse - big
    mid = rest.astype(jnp.bfloat16).astype(jnp.float32)
    row = lax.broadcasted_iota(jnp.int32, (TAIL, lse.shape[1]), 0)
    return jnp.where(row == 0, big, jnp.where(row == 1, mid, rest - mid)).astype(jnp.bfloat16)


def lse_row(tail):
    tail = tail.astype(jnp.float32)
    return tail[0:1] + tail[1:2] + tail[2:3]


def attend_kernel(counts, first_ref, k0_ref, k1_ref, v0_ref, v1_ref, *refs):
    cand = refs[-1].shape[2]
    positions, width = k0_ref.shape
    nloc = positions // BLK
    scale = 1.0 / width**0.5
    slots = [
        (x_ref, out_ref, s)
        for x_ref, out_ref, count in zip(refs, refs[-len(counts) :], counts)
        for s in range(count)
    ]
    for p in range(0, len(slots), 2):
        pair = slots[p : p + 2]
        query = jnp.concatenate([x_ref[s, :cand, :] for x_ref, _, s in pair], axis=0)
        ids = jnp.concatenate(
            [x_ref[s, cand:, :cand].astype(jnp.float32) for x_ref, _, s in pair], axis=1
        )
        parts, lses = [], []
        for half, (k_ref, v_ref) in enumerate(((k0_ref, v0_ref), (k1_ref, v1_ref))):
            near = ids - first_ref[half].astype(jnp.float32)
            inside = jnp.logical_and(near >= 0.0, near < nloc)
            sel = jnp.max(jnp.where(inside, near, -1.0), axis=0, keepdims=True)
            scores = lax.dot_general(
                k_ref[...], query, (((1,), (1,)), ((), ())), preferred_element_type=jnp.float32
            )
            picked = scores[0:BLK]
            for b in range(1, nloc):
                picked = jnp.where(sel == b, scores[b * BLK : (b + 1) * BLK], picked)
            peak = jnp.max(picked, axis=0, keepdims=True)
            expo = jnp.exp((picked - peak) * scale)
            total = jnp.sum(expo, axis=0, keepdims=True)
            spread = jnp.concatenate(
                [jnp.where(sel == b, expo, 0.0).astype(jnp.bfloat16) for b in range(nloc)], axis=0
            )
            summed = jnp.dot(v_ref[...], spread, preferred_element_type=jnp.float32)
            parts.append((summed / total).astype(jnp.bfloat16).astype(jnp.float32))
            lses.append(jnp.where(sel >= 0.0, peak * scale + jnp.log(total), NONE))
        top = jnp.maximum(lses[0], lses[1])
        mix0, mix1 = jnp.exp(lses[0] - top), jnp.exp(lses[1] - top)
        mixed = mix0 + mix1
        merged = ((mix0 / mixed) * parts[0] + (mix1 / mixed) * parts[1]).astype(jnp.bfloat16)
        tail = tail_rows(top + jnp.log(mixed))
        for j, (_, out_ref, s) in enumerate(pair):
            out_ref[s, :width, :] = merged[:, j * cand : (j + 1) * cand]
            out_ref[s, width:, :] = tail[:, j * cand : (j + 1) * cand]


def attend(first, xs, keys, vts, cand, after=()):
    counts = [x.shape[0] for x in xs]
    width = xs[0].shape[2]
    return pl.pallas_call(
        functools.partial(attend_kernel, counts),
        in_specs=[SMEM] + [VMEM] * (4 + len(xs)) + [ANY] * len(after),
        out_specs=[VMEM] * len(xs),
        out_shape=[jax.ShapeDtypeStruct((n, width + TAIL, cand), jnp.bfloat16) for n in counts],
        compiler_params=PARAMS,
    )(first, *keys, *vts, *xs, *after)


def mix(blocks):
    width = blocks[0].shape[0] - TAIL
    lses = [lse_row(one[width:, :]) for one in blocks]
    top = functools.reduce(jnp.maximum, lses)
    mixes = [jnp.exp(one - top) for one in lses]
    mixed = functools.reduce(jnp.add, mixes)
    inverse = 1.0 / mixed
    total = (mixes[0] * inverse) * blocks[0][:width, :].astype(jnp.float32)
    for one, block in zip(mixes[1:], blocks[1:]):
        total = total + (one * inverse) * block[:width, :].astype(jnp.float32)
    return total, top + jnp.log(mixed)


def near_kernel(*refs):
    *parts, out1_ref, out2_ref = refs
    width = out1_ref.shape[0] - TAIL
    for slot, out_ref in ((1, out1_ref), (2, out2_ref)):
        total, lse = mix([ref[slot] for ref in parts])
        out_ref[:width, :] = total.astype(jnp.bfloat16)
        out_ref[width:, :] = tail_rows(lse)


def near_merge(parts):
    shape = jax.ShapeDtypeStruct(parts[0].shape[1:], parts[0].dtype)
    return pl.pallas_call(
        near_kernel,
        in_specs=[VMEM] * len(parts),
        out_specs=[VMEM] * 2,
        out_shape=[shape] * 2,
        compiler_params=PARAMS,
    )(*parts)


def far_kernel(*refs):
    *parts, out_ref = refs
    total, _ = mix([ref[0] for ref in parts])
    out_ref[...] = total.T.astype(jnp.bfloat16)


def far_merge(parts):
    _, rows, cand = parts[0].shape
    return pl.pallas_call(
        far_kernel,
        in_specs=[VMEM] * len(parts),
        out_specs=VMEM,
        out_shape=jax.ShapeDtypeStruct((cand, rows - TAIL), jnp.bfloat16),
        compiler_params=PARAMS,
    )(*parts)


def body(chips, queries, hist_keys, hist_values, block_dev, block_local):
    cand, width = queries.shape
    nloc = hist_keys.shape[0] // BLK

    def shift(x, by):
        pairs = [
            (2 * z + c, 2 * ((z + by * (1 - 2 * c)) % chips) + c)
            for z in range(chips)
            for c in range(2)
        ]
        return lax.ppermute(x, ("z", "core"), pairs)

    ids = (block_dev * nloc + block_local).astype(jnp.bfloat16).T
    mine = jnp.concatenate([queries, jnp.pad(ids, ((0, 0), (0, width - cand)))], axis=0)
    up5, down5 = shift(mine, -5), shift(mine, 5)
    eight = shift(mine[None], 8)

    swap = [(0, 1), (1, 0)]
    vt = hist_values.T
    keys = (hist_keys, lax.ppermute(hist_keys, "core", swap))
    vts = (vt, lax.ppermute(vt, "core", swap))
    here = 2 * lax.axis_index("z").astype(jnp.int32)
    core = lax.axis_index("core").astype(jnp.int32)
    first = jnp.stack([here + core, here + 1 - core]) * nloc

    own = jnp.stack([mine, up5, down5])
    up2, down2 = shift(own, -2), shift(own, 2)
    up1, down1 = shift(own, -1), shift(own, 1)

    part_up2, part_down2 = attend(first, (up2, down2), keys, vts, cand)
    back = [shift(part_up2, 2), shift(part_down2, -2)]
    part_own, part_eight = attend(first, (own, eight), keys, vts, cand, (part_up2,))
    part_up1, part_down1 = attend(first, (up1, down1), keys, vts, cand, (part_eight,))
    back += [shift(part_up1, 1), shift(part_down1, -1)]
    across = shift(part_eight, 8)
    parts = [part_own] + back
    slot1, slot2 = near_merge(parts)
    return far_merge(parts + [shift(slot1, 5)[None], shift(slot2, -5)[None], across])


def solution(mesh):
    groups, pos = mesh.devices.shape
    chips = Mesh(mesh.devices.reshape(groups, pos // 2, 2), ("group", "z", "core"))
    spec = P(("group", "z", "core"), None)
    return jax.shard_map(
        functools.partial(body, pos // 2),
        mesh=chips,
        in_specs=(spec,) * 5,
        out_specs=spec,
        check_vma=False,
    )
```

```python
import functools

import jax
import jax.numpy as jnp
from jax import lax
from jax.experimental import pallas as pl
from jax.experimental.pallas import tpu as pltpu
from jax.sharding import Mesh, PartitionSpec as P

BLK = 128
NONE = -1e30
TAIL = 16
VMEM = pl.BlockSpec(memory_space=pltpu.VMEM)
SMEM = pl.BlockSpec(memory_space=pltpu.SMEM)
ANY = pl.BlockSpec(memory_space=pl.ANY)
PARAMS = pltpu.CompilerParams(vmem_limit_bytes=40 * 1024 * 1024)


def tail_rows(lse):
    big = lse.astype(jnp.bfloat16).astype(jnp.float32)
    rest = lse - big
    mid = rest.astype(jnp.bfloat16).astype(jnp.float32)
    row = lax.broadcasted_iota(jnp.int32, (TAIL, lse.shape[1]), 0)
    return jnp.where(row == 0, big, jnp.where(row == 1, mid, rest - mid)).astype(jnp.bfloat16)


def lse_row(tail):
    tail = tail.astype(jnp.float32)
    return tail[0:1] + tail[1:2] + tail[2:3]


def attend_kernel(counts, first_ref, k0_ref, k1_ref, v0_ref, v1_ref, *refs):
    cand = refs[-1].shape[2]
    positions, width = k0_ref.shape
    nloc = positions // BLK
    scale = 1.0 / width**0.5
    slots = [
        (x_ref, out_ref, s)
        for x_ref, out_ref, count in zip(refs, refs[-len(counts) :], counts)
        for s in range(count)
    ]
    for p in range(0, len(slots), 2):
        pair = slots[p : p + 2]
        query = jnp.concatenate([x_ref[s, :cand, :] for x_ref, _, s in pair], axis=0)
        ids = jnp.concatenate(
            [x_ref[s, cand:, :cand].astype(jnp.float32) for x_ref, _, s in pair], axis=1
        )
        parts, lses = [], []
        for half, (k_ref, v_ref) in enumerate(((k0_ref, v0_ref), (k1_ref, v1_ref))):
            near = ids - first_ref[half].astype(jnp.float32)
            inside = jnp.logical_and(near >= 0.0, near < nloc)
            sel = jnp.max(jnp.where(inside, near, -1.0), axis=0, keepdims=True)
            scores = lax.dot_general(
                k_ref[...], query, (((1,), (1,)), ((), ())), preferred_element_type=jnp.float32
            )
            picked = scores[0:BLK]
            for b in range(1, nloc):
                picked = jnp.where(sel == b, scores[b * BLK : (b + 1) * BLK], picked)
            peak = jnp.max(picked, axis=0, keepdims=True)
            expo = jnp.exp((picked - peak) * scale)
            total = jnp.sum(expo, axis=0, keepdims=True)
            spread = jnp.concatenate(
                [jnp.where(sel == b, expo, 0.0).astype(jnp.bfloat16) for b in range(nloc)], axis=0
            )
            summed = jnp.dot(v_ref[...], spread, preferred_element_type=jnp.float32)
            parts.append((summed / total).astype(jnp.bfloat16).astype(jnp.float32))
            lses.append(jnp.where(sel >= 0.0, peak * scale + jnp.log(total), NONE))
        top = jnp.maximum(lses[0], lses[1])
        mix0, mix1 = jnp.exp(lses[0] - top), jnp.exp(lses[1] - top)
        mixed = mix0 + mix1
        merged = ((mix0 / mixed) * parts[0] + (mix1 / mixed) * parts[1]).astype(jnp.bfloat16)
        tail = tail_rows(top + jnp.log(mixed))
        for j, (_, out_ref, s) in enumerate(pair):
            out_ref[s, :width, :] = merged[:, j * cand : (j + 1) * cand]
            out_ref[s, width:, :] = tail[:, j * cand : (j + 1) * cand]


def attend(first, xs, keys, vts, cand, after=()):
    counts = [x.shape[0] for x in xs]
    width = xs[0].shape[2]
    return pl.pallas_call(
        functools.partial(attend_kernel, counts),
        in_specs=[SMEM] + [VMEM] * (4 + len(xs)) + [ANY] * len(after),
        out_specs=[VMEM] * len(xs),
        out_shape=[jax.ShapeDtypeStruct((n, width + TAIL, cand), jnp.bfloat16) for n in counts],
        compiler_params=PARAMS,
    )(first, *keys, *vts, *xs, *after)


def mix(blocks):
    width = blocks[0].shape[0] - TAIL
    lses = [lse_row(one[width:, :]) for one in blocks]
    top = functools.reduce(jnp.maximum, lses)
    mixes = [jnp.exp(one - top) for one in lses]
    mixed = functools.reduce(jnp.add, mixes)
    inverse = 1.0 / mixed
    total = (mixes[0] * inverse) * blocks[0][:width, :].astype(jnp.float32)
    for one, block in zip(mixes[1:], blocks[1:]):
        total = total + (one * inverse) * block[:width, :].astype(jnp.float32)
    return total, top + jnp.log(mixed)


def near_kernel(slot, count, *refs):
    *parts, out_ref = refs
    width = out_ref.shape[0] - TAIL
    total, lse = mix([ref[slot if i < count else 0] for i, ref in enumerate(parts)])
    out_ref[:width, :] = total.astype(jnp.bfloat16)
    out_ref[width:, :] = tail_rows(lse)


def near_merge(slot, parts, *extra):
    return pl.pallas_call(
        functools.partial(near_kernel, slot, len(parts)),
        in_specs=[VMEM] * (len(parts) + len(extra)),
        out_specs=VMEM,
        out_shape=jax.ShapeDtypeStruct(parts[0].shape[1:], parts[0].dtype),
        compiler_params=PARAMS,
    )(*parts, *extra)


def far_kernel(*refs):
    *parts, one, two, out_ref = refs
    total, _ = mix([ref[0] for ref in parts] + [one[...], two[...]])
    out_ref[...] = total.T.astype(jnp.bfloat16)


def far_merge(parts, one, two):
    rows, cand = one.shape
    return pl.pallas_call(
        far_kernel,
        in_specs=[VMEM] * (len(parts) + 2),
        out_specs=VMEM,
        out_shape=jax.ShapeDtypeStruct((cand, rows - TAIL), jnp.bfloat16),
        compiler_params=PARAMS,
    )(*parts, one, two)


def body(chips, queries, hist_keys, hist_values, block_dev, block_local):
    cand, width = queries.shape
    nloc = hist_keys.shape[0] // BLK

    def shift(x, by):
        pairs = [
            (2 * z + c, 2 * ((z + by * (1 - 2 * c)) % chips) + c)
            for z in range(chips)
            for c in range(2)
        ]
        return lax.ppermute(x, ("z", "core"), pairs)

    ids = (block_dev * nloc + block_local).astype(jnp.bfloat16).T
    mine = jnp.concatenate([queries, jnp.pad(ids, ((0, 0), (0, width - cand)))], axis=0)
    up5, down5 = shift(mine, -5), shift(mine, 5)

    swap = [(0, 1), (1, 0)]
    vt = hist_values.T
    keys = (hist_keys, lax.ppermute(hist_keys, "core", swap))
    vts = (vt, lax.ppermute(vt, "core", swap))
    here = 2 * lax.axis_index("z").astype(jnp.int32)
    core = lax.axis_index("core").astype(jnp.int32)
    first = jnp.stack([here + core, here + 1 - core]) * nloc

    own = jnp.stack([mine, up5, down5])
    up2, down2 = shift(own, -2), shift(own, 2)
    eight = shift(up5[None], -3)
    up1, down1 = shift(own, -1), shift(own, 1)

    part_up2, part_down2 = attend(first, (up2, down2), keys, vts, cand)
    back = [shift(part_up2, 2), shift(part_down2, -2)]
    part_own, part_eight = attend(first, (own, eight), keys, vts, cand, (part_up2,))
    extra = shift(part_eight, 3)
    part_up1, part_down1 = attend(first, (up1, down1), keys, vts, cand, (part_eight,))
    back += [shift(part_up1, 1), shift(part_down1, -1)]
    parts = [part_own] + back
    two = shift(near_merge(2, parts), -5)
    one = shift(near_merge(1, parts, extra), 5)
    return far_merge(parts, one, two)


def solution(mesh):
    groups, pos = mesh.devices.shape
    chips = Mesh(mesh.devices.reshape(groups, pos // 2, 2), ("group", "z", "core"))
    spec = P(("group", "z", "core"), None)
    return jax.shard_map(
        functools.partial(body, pos // 2),
        mesh=chips,
        in_specs=(spec,) * 5,
        out_specs=spec,
        check_vma=False,
    )
```

```python
import functools

import jax
import jax.numpy as jnp
from jax import lax
from jax.experimental import pallas as pl
from jax.experimental.pallas import tpu as pltpu
from jax.sharding import Mesh, PartitionSpec as P

BLK = 128
NONE = -1e30
TAIL = 16
VMEM = pl.BlockSpec(memory_space=pltpu.VMEM)
SMEM = pl.BlockSpec(memory_space=pltpu.SMEM)
ANY = pl.BlockSpec(memory_space=pl.ANY)
PARAMS = pltpu.CompilerParams(vmem_limit_bytes=40 * 1024 * 1024)


def tail_rows(lse):
    big = lse.astype(jnp.bfloat16).astype(jnp.float32)
    rest = lse - big
    mid = rest.astype(jnp.bfloat16).astype(jnp.float32)
    row = lax.broadcasted_iota(jnp.int32, (TAIL, lse.shape[1]), 0)
    return jnp.where(row == 0, big, jnp.where(row == 1, mid, rest - mid)).astype(jnp.bfloat16)


def lse_row(tail):
    tail = tail.astype(jnp.float32)
    return tail[0:1] + tail[1:2] + tail[2:3]


def attend_kernel(counts, first_ref, k0_ref, k1_ref, v0_ref, v1_ref, *refs):
    cand = refs[-1].shape[2]
    positions, width = k0_ref.shape
    nloc = positions // BLK
    scale = 1.0 / width**0.5
    slots = [
        (x_ref, out_ref, s)
        for x_ref, out_ref, count in zip(refs, refs[-len(counts) :], counts)
        for s in range(count)
    ]
    for p in range(0, len(slots), 2):
        pair = slots[p : p + 2]
        query = jnp.concatenate([x_ref[s, :cand, :] for x_ref, _, s in pair], axis=0)
        ids = jnp.concatenate(
            [x_ref[s, cand:, :cand].astype(jnp.float32) for x_ref, _, s in pair], axis=1
        )
        parts, lses = [], []
        for half, (k_ref, v_ref) in enumerate(((k0_ref, v0_ref), (k1_ref, v1_ref))):
            near = ids - first_ref[half].astype(jnp.float32)
            inside = jnp.logical_and(near >= 0.0, near < nloc)
            sel = jnp.max(jnp.where(inside, near, -1.0), axis=0, keepdims=True)
            scores = lax.dot_general(
                k_ref[...], query, (((1,), (1,)), ((), ())), preferred_element_type=jnp.float32
            )
            picked = scores[0:BLK]
            for b in range(1, nloc):
                picked = jnp.where(sel == b, scores[b * BLK : (b + 1) * BLK], picked)
            peak = jnp.max(picked, axis=0, keepdims=True)
            expo = jnp.exp((picked - peak) * scale)
            total = jnp.sum(expo, axis=0, keepdims=True)
            spread = jnp.concatenate(
                [jnp.where(sel == b, expo, 0.0).astype(jnp.bfloat16) for b in range(nloc)], axis=0
            )
            summed = jnp.dot(v_ref[...], spread, preferred_element_type=jnp.float32)
            parts.append((summed / total).astype(jnp.bfloat16).astype(jnp.float32))
            lses.append(jnp.where(sel >= 0.0, peak * scale + jnp.log(total), NONE))
        top = jnp.maximum(lses[0], lses[1])
        mix0, mix1 = jnp.exp(lses[0] - top), jnp.exp(lses[1] - top)
        mixed = mix0 + mix1
        merged = ((mix0 / mixed) * parts[0] + (mix1 / mixed) * parts[1]).astype(jnp.bfloat16)
        tail = tail_rows(top + jnp.log(mixed))
        for j, (_, out_ref, s) in enumerate(pair):
            out_ref[s, :width, :] = merged[:, j * cand : (j + 1) * cand]
            out_ref[s, width:, :] = tail[:, j * cand : (j + 1) * cand]


def attend(first, xs, keys, vts, cand, after=()):
    counts = [x.shape[0] for x in xs]
    width = xs[0].shape[2]
    return pl.pallas_call(
        functools.partial(attend_kernel, counts),
        in_specs=[SMEM] + [VMEM] * (4 + len(xs)) + [ANY] * len(after),
        out_specs=[VMEM] * len(xs),
        out_shape=[jax.ShapeDtypeStruct((n, width + TAIL, cand), jnp.bfloat16) for n in counts],
        compiler_params=PARAMS,
    )(first, *keys, *vts, *xs, *after)


def mix(blocks):
    width = blocks[0].shape[0] - TAIL
    lses = [lse_row(one[width:, :]) for one in blocks]
    top = functools.reduce(jnp.maximum, lses)
    mixes = [jnp.exp(one - top) for one in lses]
    mixed = functools.reduce(jnp.add, mixes)
    inverse = 1.0 / mixed
    total = (mixes[0] * inverse) * blocks[0][:width, :].astype(jnp.float32)
    for one, block in zip(mixes[1:], blocks[1:]):
        total = total + (one * inverse) * block[:width, :].astype(jnp.float32)
    return total, top + jnp.log(mixed)


def near_kernel(slot, count, *refs):
    *parts, out_ref = refs
    width = out_ref.shape[0] - TAIL
    total, lse = mix([ref[slot if i < count else 0] for i, ref in enumerate(parts)])
    out_ref[:width, :] = total.astype(jnp.bfloat16)
    out_ref[width:, :] = tail_rows(lse)


def near_merge(slot, parts, *extra):
    return pl.pallas_call(
        functools.partial(near_kernel, slot, len(parts)),
        in_specs=[VMEM] * (len(parts) + len(extra)),
        out_specs=VMEM,
        out_shape=jax.ShapeDtypeStruct(parts[0].shape[1:], parts[0].dtype),
        compiler_params=PARAMS,
    )(*parts, *extra)


def far_kernel(*refs):
    *parts, one, two, out_ref = refs
    total, _ = mix([ref[0] for ref in parts] + [one[...], two[...]])
    out_ref[...] = total.T.astype(jnp.bfloat16)


def far_merge(parts, one, two):
    rows, cand = one.shape
    return pl.pallas_call(
        far_kernel,
        in_specs=[VMEM] * (len(parts) + 2),
        out_specs=VMEM,
        out_shape=jax.ShapeDtypeStruct((cand, rows - TAIL), jnp.bfloat16),
        compiler_params=PARAMS,
    )(*parts, one, two)


def body(chips, queries, hist_keys, hist_values, block_dev, block_local):
    cand, width = queries.shape
    nloc = hist_keys.shape[0] // BLK

    def shift(x, by):
        pairs = [
            (2 * z + c, 2 * ((z + by * (1 - 2 * c)) % chips) + c)
            for z in range(chips)
            for c in range(2)
        ]
        return lax.ppermute(x, ("z", "core"), pairs)

    ids = (block_dev * nloc + block_local).astype(jnp.bfloat16).T
    mine = jnp.concatenate([queries, jnp.pad(ids, ((0, 0), (0, width - cand)))], axis=0)
    up5, down5 = shift(mine, -5), shift(mine, 5)

    swap = [(0, 1), (1, 0)]
    vt = hist_values.T
    keys = (hist_keys, lax.ppermute(hist_keys, "core", swap))
    vts = (vt, lax.ppermute(vt, "core", swap))
    here = 2 * lax.axis_index("z").astype(jnp.int32)
    core = lax.axis_index("core").astype(jnp.int32)
    first = jnp.stack([here + core, here + 1 - core]) * nloc

    own = jnp.stack([mine, up5, down5])
    up2, down2 = shift(own, -2), shift(own, 2)
    eight = shift(up5[None], -3)
    up1, down1 = shift(own, -1), shift(own, 1)

    part_up2, part_down2, part_eight, part_up1, part_down1, part_own = attend(
        first, (up2, down2, eight, up1, down1, own), keys, vts, cand
    )
    back = [shift(part_up2, 2), shift(part_down2, -2), shift(part_up1, 1), shift(part_down1, -1)]
    extra = shift(part_eight, 3)
    parts = [part_own] + back
    two = shift(near_merge(2, parts), -5)
    one = shift(near_merge(1, parts, extra), 5)
    return far_merge(parts, one, two)


def solution(mesh):
    groups, pos = mesh.devices.shape
    chips = Mesh(mesh.devices.reshape(groups, pos // 2, 2), ("group", "z", "core"))
    spec = P(("group", "z", "core"), None)
    return jax.shard_map(
        functools.partial(body, pos // 2),
        mesh=chips,
        in_specs=(spec,) * 5,
        out_specs=spec,
        check_vma=False,
    )
```

```python
import functools

import jax
import jax.numpy as jnp
from jax import lax
from jax.experimental import pallas as pl
from jax.experimental.pallas import tpu as pltpu
from jax.sharding import Mesh, PartitionSpec as P

BLK = 128
NONE = -1e30
TAIL = 16
VMEM = pl.BlockSpec(memory_space=pltpu.VMEM)
SMEM = pl.BlockSpec(memory_space=pltpu.SMEM)
ANY = pl.BlockSpec(memory_space=pl.ANY)
PARAMS = pltpu.CompilerParams(vmem_limit_bytes=40 * 1024 * 1024)


def tail_rows(lse):
    big = lse.astype(jnp.bfloat16).astype(jnp.float32)
    rest = lse - big
    mid = rest.astype(jnp.bfloat16).astype(jnp.float32)
    row = lax.broadcasted_iota(jnp.int32, (TAIL, lse.shape[1]), 0)
    return jnp.where(row == 0, big, jnp.where(row == 1, mid, rest - mid)).astype(jnp.bfloat16)


def lse_row(tail):
    tail = tail.astype(jnp.float32)
    return tail[0:1] + tail[1:2] + tail[2:3]


def attend_kernel(counts, first_ref, k0_ref, k1_ref, v0_ref, v1_ref, *refs):
    cand = refs[-1].shape[2]
    positions, width = k0_ref.shape
    nloc = positions // BLK
    scale = 1.0 / width**0.5
    slots = [
        (x_ref, out_ref, s)
        for x_ref, out_ref, count in zip(refs, refs[-len(counts) :], counts)
        for s in range(count)
    ]
    for p in range(0, len(slots), 2):
        pair = slots[p : p + 2]
        query = jnp.concatenate([x_ref[s, :cand, :] for x_ref, _, s in pair], axis=0)
        ids = jnp.concatenate(
            [x_ref[s, cand:, :cand].astype(jnp.float32) for x_ref, _, s in pair], axis=1
        )
        parts, lses = [], []
        for half, (k_ref, v_ref) in enumerate(((k0_ref, v0_ref), (k1_ref, v1_ref))):
            near = ids - first_ref[half].astype(jnp.float32)
            inside = jnp.logical_and(near >= 0.0, near < nloc)
            sel = jnp.max(jnp.where(inside, near, -1.0), axis=0, keepdims=True)
            scores = lax.dot_general(
                k_ref[...], query, (((1,), (1,)), ((), ())), preferred_element_type=jnp.float32
            )
            picked = scores[0:BLK]
            for b in range(1, nloc):
                picked = jnp.where(sel == b, scores[b * BLK : (b + 1) * BLK], picked)
            peak = jnp.max(picked, axis=0, keepdims=True)
            expo = jnp.exp((picked - peak) * scale)
            total = jnp.sum(expo, axis=0, keepdims=True)
            spread = jnp.concatenate(
                [jnp.where(sel == b, expo, 0.0).astype(jnp.bfloat16) for b in range(nloc)], axis=0
            )
            summed = jnp.dot(v_ref[...], spread, preferred_element_type=jnp.float32)
            parts.append((summed / total).astype(jnp.bfloat16).astype(jnp.float32))
            lses.append(jnp.where(sel >= 0.0, peak * scale + jnp.log(total), NONE))
        top = jnp.maximum(lses[0], lses[1])
        mix0, mix1 = jnp.exp(lses[0] - top), jnp.exp(lses[1] - top)
        mixed = mix0 + mix1
        merged = ((mix0 / mixed) * parts[0] + (mix1 / mixed) * parts[1]).astype(jnp.bfloat16)
        tail = tail_rows(top + jnp.log(mixed))
        for j, (_, out_ref, s) in enumerate(pair):
            out_ref[s, :width, :] = merged[:, j * cand : (j + 1) * cand]
            out_ref[s, width:, :] = tail[:, j * cand : (j + 1) * cand]


def attend(first, xs, keys, vts, cand, after=()):
    counts = [x.shape[0] for x in xs]
    width = xs[0].shape[2]
    return pl.pallas_call(
        functools.partial(attend_kernel, counts),
        in_specs=[SMEM] + [VMEM] * (4 + len(xs)) + [ANY] * len(after),
        out_specs=[VMEM] * len(xs),
        out_shape=[jax.ShapeDtypeStruct((n, width + TAIL, cand), jnp.bfloat16) for n in counts],
        compiler_params=PARAMS,
    )(first, *keys, *vts, *xs, *after)


def mix(blocks):
    width = blocks[0].shape[0] - TAIL
    lses = [lse_row(one[width:, :]) for one in blocks]
    top = functools.reduce(jnp.maximum, lses)
    mixes = [jnp.exp(one - top) for one in lses]
    mixed = functools.reduce(jnp.add, mixes)
    inverse = 1.0 / mixed
    total = (mixes[0] * inverse) * blocks[0][:width, :].astype(jnp.float32)
    for one, block in zip(mixes[1:], blocks[1:]):
        total = total + (one * inverse) * block[:width, :].astype(jnp.float32)
    return total, top + jnp.log(mixed)


def near_kernel(slot, count, *refs):
    *parts, out_ref = refs
    width = out_ref.shape[0] - TAIL
    total, lse = mix([ref[slot if i < count else 0] for i, ref in enumerate(parts)])
    out_ref[:width, :] = total.astype(jnp.bfloat16)
    out_ref[width:, :] = tail_rows(lse)


def near_merge(slot, parts, *extra):
    return pl.pallas_call(
        functools.partial(near_kernel, slot, len(parts)),
        in_specs=[VMEM] * (len(parts) + len(extra)),
        out_specs=VMEM,
        out_shape=jax.ShapeDtypeStruct(parts[0].shape[1:], parts[0].dtype),
        compiler_params=PARAMS,
    )(*parts, *extra)


def far_kernel(*refs):
    *parts, one, two, out_ref = refs
    total, _ = mix([ref[0] for ref in parts] + [one[...], two[...]])
    out_ref[...] = total.T.astype(jnp.bfloat16)


def far_merge(parts, one, two):
    rows, cand = one.shape
    return pl.pallas_call(
        far_kernel,
        in_specs=[VMEM] * (len(parts) + 2),
        out_specs=VMEM,
        out_shape=jax.ShapeDtypeStruct((cand, rows - TAIL), jnp.bfloat16),
        compiler_params=PARAMS,
    )(*parts, one, two)


def body(chips, queries, hist_keys, hist_values, block_dev, block_local):
    cand, width = queries.shape
    nloc = hist_keys.shape[0] // BLK

    def shift(x, by):
        pairs = [
            (2 * z + c, 2 * ((z + by * (1 - 2 * c)) % chips) + c)
            for z in range(chips)
            for c in range(2)
        ]
        return lax.ppermute(x, ("z", "core"), pairs)

    ids = (block_dev * nloc + block_local).astype(jnp.bfloat16).T
    mine = jnp.concatenate([queries, jnp.pad(ids, ((0, 0), (0, width - cand)))], axis=0)
    up5, down5 = shift(mine, -5), shift(mine, 5)

    swap = [(0, 1), (1, 0)]
    vt = hist_values.T
    keys = (hist_keys, lax.ppermute(hist_keys, "core", swap))
    vts = (vt, lax.ppermute(vt, "core", swap))
    here = 2 * lax.axis_index("z").astype(jnp.int32)
    core = lax.axis_index("core").astype(jnp.int32)
    first = jnp.stack([here + core, here + 1 - core]) * nloc

    own = jnp.stack([mine, up5, down5])
    up2, down2 = shift(own, -2), shift(own, 2)
    eight = shift(up5[None], -3)
    up1, down1 = shift(own, -1), shift(own, 1)

    part_up2, part_down2, part_eight, part_up1, part_down1 = attend(
        first, (up2, down2, eight, up1, down1), keys, vts, cand
    )
    (part_own,) = attend(first, (own,), keys, vts, cand)
    back = [shift(part_up2, 2), shift(part_down2, -2), shift(part_up1, 1), shift(part_down1, -1)]
    extra = shift(part_eight, 3)
    parts = [part_own] + back
    two = shift(near_merge(2, parts), -5)
    one = shift(near_merge(1, parts, extra), 5)
    return far_merge(parts, one, two)


def solution(mesh):
    groups, pos = mesh.devices.shape
    chips = Mesh(mesh.devices.reshape(groups, pos // 2, 2), ("group", "z", "core"))
    spec = P(("group", "z", "core"), None)
    return jax.shard_map(
        functools.partial(body, pos // 2),
        mesh=chips,
        in_specs=(spec,) * 5,
        out_specs=spec,
        check_vma=False,
    )
```
